128 devices in a mesh: dp: 16 (over y, x), tensor: 8 (over z, core).
Axes of the slice: x: 4, y: 4, z: 4, core: 2. Of those that a mesh axis runs over, the one named last changes fastest.
Arguments:
- acts: bfloat16 [16384, 5120], P('dp'), may hold values from -12 to 12
- out_grad: bfloat16 [16384, 5120], P('dp', 'tensor'), may hold values from -0.0625 to 0.0625
- error: bfloat16 [81920, 5120], P('dp', 'tensor'), may hold values from -9 to 9
- q_seed: int32 [5120, 32], P('tensor'), may hold values from -64 to 64
- dither: int32 [5120, 32], P('tensor'), may hold values from 0 to 65535
Outputs:
- q_factor: bfloat16 [5120, 32], P('tensor')
- new_error: bfloat16 [81920, 5120], P('dp', 'tensor')
The draws below stay inside these ranges and needn't reach their ends.
All inputs are finite; a program needn't handle non-finite values.
Results may differ from the reference program's by a relative error of at most 0.0053.
Values sent between devices are 32-bit elements; how exact they have to be, the bound alone decides.
No kernel may reach another device: no remote copies, remote signals or barrier semaphores. Data moves between devices by JAX's collectives and lax.ppermute only.
A program may use at most 128 MiB of HBM per device.

```python
import math
import jax
import jax.numpy as jnp
from jax import lax

D = 5120
RANK = 32
TOK_DEV = 1024
TOKENS = 16384
EROWS = 81920
N_DP = 16


HIGH = lax.Precision.HIGHEST


def shared_parts(key):
    rank_half = RANK // 2
    token_signs = (jax.random.randint(jax.random.fold_in(key, 101), (TOKENS, rank_half), 0, 2) * 2 - 1).astype(jnp.float32)
    left_dirs = jax.random.randint(jax.random.fold_in(key, 102), (rank_half, D), -12, 13).astype(jnp.float32) / 32.0
    right_dirs = jax.random.randint(jax.random.fold_in(key, 103), (rank_half, D), -12, 13).astype(jnp.float32) / 32.0
    return (token_signs, left_dirs, right_dirs)


def draw_acts(key, part):
    token_signs, left_dirs, right_dirs = shared_parts(key)
    key = jax.random.fold_in(key, 1)
    noise_part = jax.random.truncated_normal(key, -4.0, 4.0, (TOKENS, D), jnp.float32)
    strength = 1.0
    low_rank = jnp.dot(token_signs, left_dirs, precision=HIGH)
    return (noise_part + strength * low_rank).astype(jnp.bfloat16)


def draw_out_grad(key, part):
    token_signs, left_dirs, right_dirs = shared_parts(key)
    key = jax.random.fold_in(key, 2)
    noise_part = jax.random.truncated_normal(key, -4.0, 4.0, (TOKENS, D), jnp.float32)
    strength = 1.0
    low_rank = jnp.dot(token_signs, right_dirs, precision=HIGH)
    scale_noise = 0.25 / math.sqrt(TOK_DEV)
    scale_low = 2.0 * strength / TOK_DEV
    return (scale_noise * noise_part + scale_low * low_rank).astype(jnp.bfloat16)


def draw_error(key, part):
    token_signs, left_dirs, right_dirs = shared_parts(key)
    key = jax.random.fold_in(key, 3)
    workers = EROWS // D
    rank_half = RANK // 2
    strengths = jax.random.randint(jax.random.fold_in(key, 11), (workers, rank_half), -2, 3).astype(jnp.float32)
    noise_key = jax.random.fold_in(key, 12)
    scale_low = 0.75

    def one_worker(index):
        worker_key = jax.random.fold_in(noise_key, index)
        noise_part = jax.random.truncated_normal(worker_key, -4.0, 4.0, (D, D), jnp.float32)
        scaled = left_dirs.T * strengths[index][None, :]
        low_rank = jnp.dot(scaled, right_dirs, precision=HIGH)
        return (0.25 * noise_part + scale_low * low_rank).astype(jnp.bfloat16)
    blocks = lax.map(one_worker, jnp.arange(workers, dtype=jnp.int32))
    return blocks.reshape(EROWS, D)


def touch_ends(values, own_key, smallest, high):
    longest = values.shape.index(max(values.shape))
    spots = []
    for shift in (0, 1):
        where = [jax.random.randint(jax.random.fold_in(own_key, axis), (), 0, length) for axis, length in enumerate(values.shape)]
        where[longest] = (where[longest] + shift) % values.shape[longest]
        spots.append(tuple(where))
    return values.at[spots[0]].set(smallest).at[spots[1]].set(high)


def setup_inputs(seed: int = 0) -> dict:
    streams_of = jax.random.split(jax.random.key(seed), 6)
    acts = draw_acts(jax.random.fold_in(streams_of[5], 71), 0)
    out_grad = draw_out_grad(jax.random.fold_in(streams_of[5], 71), 0)
    error = draw_error(jax.random.fold_in(streams_of[5], 71), 0)
    q_seed = touch_ends(jax.random.randint(streams_of[3], (D, RANK), -64, 65), jax.random.fold_in(streams_of[3], 1), -64, 64).astype(jnp.int32)
    dither = touch_ends(jax.random.randint(streams_of[4], (D, RANK), 0, 65536), jax.random.fold_in(streams_of[4], 1), 0, 65535).astype(jnp.int32)
    return dict(acts=acts, out_grad=out_grad, error=error, q_seed=q_seed, dither=dither)


HIGH = lax.Precision.HIGHEST

def reference(acts, out_grad, error, q_seed, dither):
    q_start = q_seed.astype(jnp.float32) / 32.0
    blocks_x = acts.reshape(N_DP, TOK_DEV, D)
    blocks_g = out_grad.reshape(N_DP, TOK_DEV, D)
    blocks_e = error.reshape(N_DP, D, D)

    def left_term(carry, items):
        xb, gb, eb = items
        tmp = jnp.dot(gb.astype(jnp.float32), q_start, precision=HIGH)
        term = jnp.dot(xb.astype(jnp.float32).T, tmp, precision=HIGH)
        term = term + jnp.dot(eb.astype(jnp.float32), q_start, precision=HIGH)
        return (carry + term, None)
    pmat, _ = lax.scan(left_term, jnp.zeros((D, RANK), jnp.float32), (blocks_x, blocks_g, blocks_e))
    gram = jnp.dot(pmat.T, pmat, precision=HIGH)
    lower = jnp.linalg.cholesky(gram)
    p_hat = lax.linalg.triangular_solve(lower, pmat, left_side=False, lower=True, transpose_a=True)

    def right_term(carry, items):
        xb, gb, eb = items
        tmp = jnp.dot(xb.astype(jnp.float32), p_hat, precision=HIGH)
        term = jnp.dot(gb.astype(jnp.float32).T, tmp, precision=HIGH)
        term = term + jnp.dot(eb.astype(jnp.float32).T, p_hat, precision=HIGH)
        return (carry + term, None)
    qsum, _ = lax.scan(right_term, jnp.zeros((D, RANK), jnp.float32), (blocks_x, blocks_g, blocks_e))
    qmat = qsum / N_DP
    q_factor = (qmat * (1.0 + (dither.astype(jnp.float32) / 65536.0 - 0.5) / 4.0)).astype(jnp.bfloat16)
    approx = jnp.dot(p_hat, q_factor.astype(jnp.float32).T, precision=HIGH)

    def update(items):
        xb, gb, eb = items
        grad = lax.dot_general(xb.astype(jnp.float32), gb.astype(jnp.float32), (((0,), (0,)), ((), ())), preferred_element_type=jnp.float32)
        return (grad + eb.astype(jnp.float32) - approx).astype(jnp.bfloat16)
    new_error = lax.map(update, (blocks_x, blocks_g, blocks_e))
    return (q_factor, new_error.reshape(N_DP * D, D))
```

```python
import jax
import jax.numpy as jnp
from jax import lax
from jax.experimental import pallas as pl
from jax.experimental.pallas import tpu as pltpu
from jax.sharding import PartitionSpec as P

HIGH = lax.Precision.HIGHEST
F32 = jnp.float32
BF16 = jnp.bfloat16

D = 5120
TOK = 1024
COLS = 640
RANK = 32
NBLK = 8
WORKERS = 16
MB = 1 << 20

NT = (((1,), (1,)), ((), ()))
TN = (((0,), (0,)), ((), ()))


def params(mb, n=1):
    return pltpu.CompilerParams(
        vmem_limit_bytes=mb * MB, dimension_semantics=("arbitrary",) * n
    )


def split3(x):
    hi = x.astype(BF16)
    r = x - hi.astype(F32)
    mid = r.astype(BF16)
    lo = (r - mid.astype(F32)).astype(BF16)
    return jnp.concatenate([hi, mid, lo], axis=0)


def fold3(y):
    return y[:RANK] + y[RANK : 2 * RANK] + y[2 * RANK :]


def left_body(first, t_ref, acts_ref, err_ref, grad_ref, seed_ref, t3_in, *outs):
    if first:
        p_ref, t3_ref, qt_ref = outs

        @pl.when(pl.program_id(0) == 0)
        def _():
            qt = seed_ref[...].astype(F32).T.astype(BF16)
            qt_ref[...] = qt
            tt = lax.dot_general(qt, grad_ref[...], NT, preferred_element_type=F32)
            t3_ref[...] = split3(tt)

        t3 = t3_ref[...]
        qt = qt_ref[...]
    else:
        (p_ref,) = outs
        t3 = t3_in[...]
        qt = seed_ref[...]
    p = fold3(jnp.dot(t3, acts_ref[...], preferred_element_type=F32))
    p = p + lax.dot_general(qt, err_ref[...], NT, preferred_element_type=F32)
    p_ref[0] = p * (1.0 / 32.0)


def left_first(t, acts, error, out_grad, q_seed):
    def body(t_ref, a, e, g, s, *outs):
        left_body(True, t_ref, a, e, g, s, None, *outs)

    return pl.pallas_call(
        body,
        out_shape=(
            jax.ShapeDtypeStruct((4, RANK, COLS), F32),
            jax.ShapeDtypeStruct((3 * RANK, TOK), BF16),
            jax.ShapeDtypeStruct((RANK, COLS), BF16),
        ),
        grid_spec=pltpu.PrefetchScalarGridSpec(
            num_scalar_prefetch=1,
            grid=(4,),
            in_specs=[
                pl.BlockSpec((TOK, COLS), lambda i, t: (0, t[0] ^ (2 * i + 1))),
                pl.BlockSpec((COLS, COLS), lambda i, t: (t[0] ^ (2 * i + 1), 0)),
                pl.BlockSpec((TOK, COLS), lambda i, t: (0, 0)),
                pl.BlockSpec((COLS, RANK), lambda i, t: (0, 0)),
            ],
            out_specs=[
                pl.BlockSpec((1, RANK, COLS), lambda i, t: (i, 0, 0)),
                pl.BlockSpec((3 * RANK, TOK), lambda i, t: (0, 0)),
                pl.BlockSpec((RANK, COLS), lambda i, t: (0, 0)),
            ],
        ),
        compiler_params=params(24),
        cost_estimate=pl.CostEstimate(
            flops=2 * 4 * 256 * COLS * (TOK + COLS), bytes_accessed=10 * MB, transcendentals=0
        ),
        name="left_first",
    )(t, acts, error, out_grad, q_seed)


def left_second(t, acts, error, t3, qt):
    def body(t_ref, a, e, s, t3_in, *outs):
        left_body(False, t_ref, a, e, None, s, t3_in, *outs)

    return pl.pallas_call(
        body,
        out_shape=jax.ShapeDtypeStruct((4, RANK, COLS), F32),
        grid_spec=pltpu.PrefetchScalarGridSpec(
            num_scalar_prefetch=1,
            grid=(4,),
            in_specs=[
                pl.BlockSpec((TOK, COLS), lambda i, t: (0, t[0] ^ (2 * i))),
                pl.BlockSpec((COLS, COLS), lambda i, t: (t[0] ^ (2 * i), 0)),
                pl.BlockSpec((RANK, COLS), lambda i, t: (0, 0)),
                pl.BlockSpec((3 * RANK, TOK), lambda i, t: (0, 0)),
            ],
            out_specs=pl.BlockSpec((1, RANK, COLS), lambda i, t: (i, 0, 0)),
        ),
        compiler_params=params(24),
        cost_estimate=pl.CostEstimate(
            flops=2 * 4 * 256 * COLS * (TOK + COLS), bytes_accessed=9 * MB, transcendentals=0
        ),
        name="left_second",
    )(t, acts, error, qt, t3)


def memory_part(first, count, acts, out_grad, error, held):
    def body(a_ref, g_ref, e_ref, *rest):
        out_ref = rest[-1]
        grad = lax.dot_general(a_ref[...], g_ref[...], TN, preferred_element_type=F32)
        out_ref[...] = grad + e_ref[...].astype(F32)

    in_specs = [
        pl.BlockSpec((TOK, COLS), lambda i: (0, first + i)),
        pl.BlockSpec((TOK, COLS), lambda i: (0, 0)),
        pl.BlockSpec((COLS, COLS), lambda i: (first + i, 0)),
    ]
    args = [acts, out_grad, error]
    aliases = {}
    if held is not None:
        in_specs.append(pl.BlockSpec(memory_space=pl.ANY))
        args.append(held)
        aliases = {3: 0}
    return pl.pallas_call(
        body,
        out_shape=jax.ShapeDtypeStruct((D, COLS), F32),
        grid=(count,),
        in_specs=in_specs,
        out_specs=pl.BlockSpec((COLS, COLS), lambda i: (first + i, 0)),
        input_output_aliases=aliases,
        compiler_params=params(24),
        cost_estimate=pl.CostEstimate(
            flops=2 * count * COLS * COLS * TOK, bytes_accessed=count * 4 * MB, transcendentals=0
        ),
        name="memory_part",
    )(*args)


def right_body(last, t_ref, acts_ref, err_ref, grad_ref, *rest):
    blocks = rest[:4]
    if last:
        tmp_in, q_in, q_ref, p3, tmp = rest[4:]
    else:
        tmp, q_ref, p3 = rest[4:]
    i = pl.program_id(0)

    @pl.when(i == 0)
    def _():
        for k in range(4):
            p3[k] = split3(blocks[k][...])
        if last:
            tmp[...] = tmp_in[...]
            q_ref[...] = q_in[...]
        else:
            tmp[...] = jnp.zeros_like(tmp)
            q_ref[...] = jnp.zeros_like(q_ref)

    p = p3[i]
    tmp[...] += fold3(lax.dot_general(p, acts_ref[...], NT, preferred_element_type=F32))
    q_ref[...] += fold3(jnp.dot(p, err_ref[...], preferred_element_type=F32))
    if last:

        @pl.when(i == 3)
        def _():
            t3 = split3(tmp[...])
            q_ref[...] += fold3(jnp.dot(t3, grad_ref[...], preferred_element_type=F32))


def right_part(last, t, acts, error, out_grad, blocks, tmp=None, q=None):
    rc = 1 if last else 0

    def whole(*shape):
        return pl.BlockSpec(shape, lambda i, t: (0,) * len(shape))

    in_specs = [
        pl.BlockSpec((TOK, COLS), lambda i, t: (0, t[0] ^ (2 * i + rc))),
        pl.BlockSpec((COLS, COLS), lambda i, t: (t[0] ^ (2 * i + rc), 0)),
        whole(TOK, COLS),
    ] + [whole(RANK, COLS)] * 4
    args = [acts, error, out_grad, *blocks]
    scratch = [pltpu.VMEM((4, 3 * RANK, COLS), BF16)]
    q_shape = jax.ShapeDtypeStruct((RANK, COLS), F32)
    tmp_shape = jax.ShapeDtypeStruct((RANK, TOK), F32)
    if last:
        in_specs += [whole(RANK, TOK), whole(RANK, COLS)]
        args += [tmp, q]
        scratch.append(pltpu.VMEM((RANK, TOK), F32))
        out_shape, out_specs = q_shape, whole(RANK, COLS)
    else:
        out_shape, out_specs = (tmp_shape, q_shape), [whole(RANK, TOK), whole(RANK, COLS)]

    def body(*refs):
        right_body(last, *refs)

    return pl.pallas_call(
        body,
        out_shape=out_shape,
        grid_spec=pltpu.PrefetchScalarGridSpec(
            num_scalar_prefetch=1,
            grid=(4,),
            in_specs=in_specs,
            out_specs=out_specs,
            scratch_shapes=scratch,
        ),
        compiler_params=params(24),
        cost_estimate=pl.CostEstimate(
            flops=2 * 4 * 256 * COLS * (TOK + COLS), bytes_accessed=10 * MB, transcendentals=0
        ),
        name="right_last" if last else "right_first",
    )(t, *args)


def orthonormal_body(*refs):
    blocks = refs[:NBLK]
    p3_ref, inv_ref = refs[NBLK:]
    gram = jnp.zeros((RANK, RANK), F32)
    for b in blocks:
        x = b[...]
        gram = gram + lax.dot_general(x, x, NT, precision=HIGH, preferred_element_type=F32)
    rows = lax.broadcasted_iota(jnp.int32, (RANK, RANK), 0)
    cols = lax.broadcasted_iota(jnp.int32, (RANK, RANK), 1)
    eye = (rows == cols).astype(F32)
    work = jnp.concatenate([gram, eye], axis=1)
    below = lax.broadcasted_iota(jnp.int32, (RANK, 1), 0)
    for k in range(RANK):
        row = work[k : k + 1, :]
        factor = jnp.where(below > k, work[:, k : k + 1] / row[:, k : k + 1], 0.0)
        work = work - factor * row
    diag = jnp.sum(work[:, :RANK] * eye, axis=1, keepdims=True)
    inv = work[:, RANK:] / jnp.sqrt(diag)
    inv_ref[...] = inv
    for k in range(NBLK):
        p = jnp.dot(inv, blocks[k][...], precision=HIGH, preferred_element_type=F32)
        hi = p.astype(BF16).astype(F32)
        r = p - hi
        mid = r.astype(BF16).astype(F32)
        stacked = jnp.concatenate([hi, mid, r - mid, jnp.zeros_like(p)], axis=0)
        p3_ref[k] = stacked.T.astype(BF16)


def orthonormal(blocks):
    return pl.pallas_call(
        orthonormal_body,
        out_shape=(
            jax.ShapeDtypeStruct((NBLK, COLS, 4 * RANK), BF16),
            jax.ShapeDtypeStruct((RANK, RANK), F32),
        ),
        compiler_params=pltpu.CompilerParams(vmem_limit_bytes=24 * MB),
        cost_estimate=pl.CostEstimate(flops=1 << 31, bytes_accessed=2 * MB, transcendentals=0),
        name="orthonormal",
    )(*blocks)


def update_body(t_ref, a_ref, b_ref, inv_ref, dither_ref, p3_ref, mem_ref, qf_ref, out_ref, q3):
    @pl.when(pl.program_id(0) == 0)
    def _():
        total = a_ref[...] + b_ref[...]
        qmat = jnp.dot(inv_ref[...], total, precision=HIGH, preferred_element_type=F32) / WORKERS
        scale = 1.0 + (dither_ref[...].astype(F32) / 65536.0 - 0.5) / 4.0
        qt = (qmat * scale.T).astype(BF16)
        for k in range(3):
            q3[k * RANK : (k + 1) * RANK, :] = qt
        q3[3 * RANK :, :] = jnp.zeros((RANK, COLS), BF16)
        qf_ref[...] = qt.astype(F32).T.astype(BF16)

    approx = jnp.dot(p3_ref[0], q3[...], preferred_element_type=F32)
    out_ref[...] = (mem_ref[...] - approx).astype(BF16)


def update(t, part_a, part_b, inv, dither, p3, memory):
    def whole(*shape):
        return pl.BlockSpec(shape, lambda i, t: (0,) * len(shape))

    return pl.pallas_call(
        update_body,
        out_shape=(
            jax.ShapeDtypeStruct((COLS, RANK), BF16),
            jax.ShapeDtypeStruct((D, COLS), BF16),
        ),
        grid_spec=pltpu.PrefetchScalarGridSpec(
            num_scalar_prefetch=1,
            grid=(NBLK,),
            in_specs=[
                whole(RANK, COLS),
                whole(RANK, COLS),
                whole(RANK, RANK),
                whole(COLS, RANK),
                pl.BlockSpec((1, COLS, 4 * RANK), lambda i, t: (t[0] ^ i, 0, 0)),
                pl.BlockSpec((COLS, COLS), lambda i, t: (i, 0)),
            ],
            out_specs=[
                whole(COLS, RANK),
                pl.BlockSpec((COLS, COLS), lambda i, t: (i, 0)),
            ],
            scratch_shapes=[pltpu.VMEM((4 * RANK, COLS), BF16)],
        ),
        compiler_params=params(24),
        cost_estimate=pl.CostEstimate(
            flops=2 * D * COLS * 256, bytes_accessed=20 * MB, transcendentals=0
        ),
        name="update",
    )(t, part_a, part_b, inv, dither, p3, memory)


def swap(x, axis, size, mask):
    return lax.ppermute(x, axis, [(i, i ^ mask) for i in range(size)])


def per_device(acts, out_grad, error, q_seed, dither):
    t = lax.axis_index("tensor").astype(jnp.int32).reshape(1)

    def over_tensor(x, mask):
        return swap(x, "tensor", NBLK, mask)

    def over_dp(x, mask):
        return swap(x, "dp", WORKERS, mask)

    away, t3, qt = left_first(t, acts, error, out_grad, q_seed)
    came = over_tensor(away, 1)
    kept = left_second(t, acts, error, t3, qt)
    part = kept + came
    from_z = [over_tensor(part[r], 2 * r) for r in (1, 2, 3)]
    own = part[0] + from_z[0] + from_z[1] + from_z[2]
    memory = None
    for first in range(0, NBLK, 2):
        memory = memory_part(first, 2, acts, out_grad, error, memory)
    for mask in (1, 3, 4, 12):
        own = own + over_dp(own, mask)

    mine = [own] + [over_tensor(own, 2 * r) for r in (1, 2, 3)]
    theirs = [over_tensor(x, 1) for x in mine]
    tmp, q = right_part(False, t, acts, error, out_grad, mine)
    q = right_part(True, t, acts, error, out_grad, theirs, tmp, q)

    blocks = [b for pair in zip(mine, theirs) for b in pair]
    p3, inv = orthonormal(blocks)
    for mask in (1, 3, 4):
        q = q + over_dp(q, mask)
    last = over_dp(q, 12)
    q_factor, new_error = update(t, q, last, inv, dither, p3, memory)
    return (q_factor, new_error)


def solution(mesh):
    in_specs = (
        P("dp", None),
        P("dp", "tensor"),
        P("dp", "tensor"),
        P("tensor", None),
        P("tensor", None),
    )
    out_specs = (P("tensor", None), P("dp", "tensor"))
    return jax.shard_map(
        per_device, mesh=mesh, in_specs=in_specs, out_specs=out_specs, check_vma=False
    )
```

```python
import jax
import jax.numpy as jnp
from jax import lax
from jax.experimental import pallas as pl
from jax.experimental.pallas import tpu as pltpu
from jax.sharding import PartitionSpec as P

HIGH = lax.Precision.HIGHEST
F32 = jnp.float32
BF16 = jnp.bfloat16

D = 5120
TOK = 1024
COLS = 640
RANK = 32
TRI = 3 * RANK
NBLK = 8
HALF = 4
WORKERS = 16
MB = 1 << 20
RING = (1, 3, 2)

NT = (((1,), (1,)), ((), ()))
TN = (((0,), (0,)), ((), ()))

VM = pl.BlockSpec(memory_space=pltpu.VMEM)
SM = pl.BlockSpec(memory_space=pltpu.SMEM)
ANY = pl.BlockSpec(memory_space=pl.ANY)


def params(mb):
    return pltpu.CompilerParams(vmem_limit_bytes=mb * MB)


def cost(flops, bytes_accessed=0):
    return pl.CostEstimate(flops=flops, bytes_accessed=bytes_accessed, transcendentals=0)


def split3(x):
    hi = x.astype(BF16)
    r = x - hi.astype(F32)
    mid = r.astype(BF16)
    lo = (r - mid.astype(F32)).astype(BF16)
    return jnp.concatenate([hi, mid, lo], axis=0)


def fold3(y):
    return y[:RANK] + y[RANK : 2 * RANK] + y[2 * RANK :]


def left(rc, t, acts, error, out_grad, q_seed, t3=None, qt=None):
    first = t3 is None

    def body(t_ref, acts_hbm, err_hbm, grad_in, seed_in, *rest):
        if first:
            p_ref, acts_v, err_v, grad_v, t3_ref, qt_ref, sem, gsem = rest
        else:
            t3_ref, p_ref, acts_v, err_v, sem = rest
            qt_ref = seed_in

        def columns(k):
            return pl.ds(pl.multiple_of((t_ref[0] ^ (2 * k + rc)) * COLS, COLS), COLS)

        acts_copy = [
            pltpu.make_async_copy(acts_hbm.at[:, columns(k)], acts_v.at[k], sem.at[0, k])
            for k in range(HALF)
        ]
        err_copy = [
            pltpu.make_async_copy(err_hbm.at[columns(k), :], err_v.at[k], sem.at[1, k])
            for k in range(HALF)
        ]
        if first:
            grad_copy = pltpu.make_async_copy(grad_in, grad_v, gsem)
            grad_copy.start()
            err_copy[0].start()
            err_copy[1].start()
            qt_ref[...] = seed_in[...].astype(F32).astype(BF16)
            grad_copy.wait()
            err_copy[2].start()
            err_copy[3].start()
            acts_copy[0].start()
            tt = lax.dot_general(qt_ref[...], grad_v[...], NT, preferred_element_type=F32)
            t3_ref[...] = split3(tt)
        else:
            for k in range(HALF):
                err_copy[k].start()
            acts_copy[0].start()
        for k in range(HALF):
            err_copy[k].wait()
            if k + 1 < HALF:
                acts_copy[k + 1].start()
            p_ref[k] = lax.dot_general(qt_ref[...], err_v[k], NT, preferred_element_type=F32)
        for k in range(HALF):
            acts_copy[k].wait()
            p = fold3(jnp.dot(t3_ref[...], acts_v[k], preferred_element_type=F32))
            p_ref[k] = (p + p_ref[k]) * (1.0 / 32.0)

    out_shape = [
        jax.ShapeDtypeStruct((HALF, RANK, COLS), F32),
        pltpu.VMEM((HALF, TOK, COLS), BF16),
        pltpu.VMEM((HALF, COLS, COLS), BF16),
    ]
    scratch = [pltpu.SemaphoreType.DMA((2, HALF))]
    if first:
        out_shape += [
            pltpu.VMEM((TOK, COLS), BF16),
            pltpu.VMEM((TRI, TOK), BF16),
            pltpu.VMEM((RANK, COLS), BF16),
        ]
        scratch.append(pltpu.SemaphoreType.DMA)
        args = (t, acts, error, out_grad, q_seed)
        in_specs = [SM, ANY, ANY, ANY, VM]
    else:
        args = (t, acts, error, out_grad, qt, t3)
        in_specs = [SM, ANY, ANY, VM, VM, VM]
    return pl.pallas_call(
        body,
        out_shape=out_shape,
        in_specs=in_specs,
        out_specs=[VM] * len(out_shape),
        scratch_shapes=scratch,
        compiler_params=params(44 if first else 40),
        cost_estimate=cost(2 * HALF * 256 * COLS * (TOK + COLS), 9 * MB),
        name="left_first" if first else "left_second",
    )(*args)


def memory_blocks(ks, half, grad_v, after):
    def body(a_ref, e_ref, g_ref, after_ref, *outs):
        for k, out_ref in zip(ks, outs):
            grad = lax.dot_general(a_ref[k], g_ref[...], TN, preferred_element_type=F32)
            out_ref[...] = grad + e_ref[k].astype(F32)

    return pl.pallas_call(
        body,
        out_shape=[pltpu.VMEM((COLS, COLS), F32)] * len(ks),
        in_specs=[VM, VM, VM, ANY],
        out_specs=[VM] * len(ks),
        compiler_params=params(8),
        cost_estimate=cost(2 * len(ks) * COLS * COLS * TOK),
        name="memory_blocks",
    )(*half, grad_v, after)


def right(work, grad_v, halves, earlier=(), last=False):
    n, m = len(work), len(earlier)

    def body(a0, e0, a1, e1, g_ref, *rest):
        acts_v, err_v = (a0, a1), (e0, e1)
        blocks, rest = rest[:n], rest[n:]
        given, outs = rest[: 3 * m], rest[3 * m :]
        tmp = q = gram = 0.0
        for (h, k, _), block in zip(work, blocks):
            p = split3(block[...])
            tmp = tmp + fold3(lax.dot_general(p, acts_v[h][k], NT, preferred_element_type=F32))
            q = q + fold3(jnp.dot(p, err_v[h][k], preferred_element_type=F32))
            gram = gram + lax.dot_general(p, p, NT, preferred_element_type=F32)
        for i in range(m):
            tmp = tmp + given[3 * i][...]
            q = q + given[3 * i + 1][...]
            gram = gram + given[3 * i + 2][...]
        if last:
            q = q + fold3(jnp.dot(split3(tmp), g_ref[...], preferred_element_type=F32))
            outs[0][...] = q
            outs[1][...] = gram
        else:
            outs[0][...] = tmp
            outs[1][...] = q
            outs[2][...] = gram

    shapes = [
        jax.ShapeDtypeStruct((RANK, TOK), F32),
        jax.ShapeDtypeStruct((RANK, COLS), F32),
        jax.ShapeDtypeStruct((TRI, TRI), F32),
    ]
    if last:
        shapes = shapes[1:]
    args = [*halves[0], *halves[1], grad_v, *(b for _, _, b in work), *(x for e in earlier for x in e)]
    return pl.pallas_call(
        body,
        out_shape=shapes,
        in_specs=[VM] * len(args),
        out_specs=[VM] * len(shapes),
        compiler_params=params(8),
        cost_estimate=cost(2 * n * 256 * COLS * (TOK + COLS)),
        name="right_last" if last else "right_part",
    )(*args)


def orthonormal_body(gram_ref, *refs):
    blocks = refs[:NBLK]
    p3_ref, inv_ref = refs[NBLK:]
    wide = fold3(gram_ref[...])
    gram = wide[:, :RANK] + wide[:, RANK : 2 * RANK] + wide[:, 2 * RANK :]
    rows = lax.broadcasted_iota(jnp.int32, (RANK, RANK), 0)
    cols = lax.broadcasted_iota(jnp.int32, (RANK, RANK), 1)
    eye = (rows == cols).astype(F32)
    work = jnp.concatenate([gram, eye], axis=1)
    below = lax.broadcasted_iota(jnp.int32, (RANK, 1), 0)
    for k in range(RANK):
        row = work[k : k + 1, :]
        factor = jnp.where(below > k, work[:, k : k + 1] / row[:, k : k + 1], 0.0)
        work = work - factor * row
    diag = jnp.sum(work[:, :RANK] * eye, axis=1, keepdims=True)
    inv = work[:, RANK:] / jnp.sqrt(diag)
    inv_ref[...] = inv
    for k in range(NBLK):
        p = jnp.dot(inv, blocks[k][...], precision=HIGH, preferred_element_type=F32)
        hi = p.astype(BF16).astype(F32)
        r = p - hi
        mid = r.astype(BF16).astype(F32)
        stacked = jnp.concatenate([hi, mid, r - mid, jnp.zeros_like(p)], axis=0)
        p3_ref[k] = stacked.T.astype(BF16)


def orthonormal(gram, blocks):
    return pl.pallas_call(
        orthonormal_body,
        out_shape=(
            pltpu.VMEM((NBLK, COLS, 4 * RANK), BF16),
            jax.ShapeDtypeStruct((RANK, RANK), F32),
        ),
        in_specs=[VM] * (1 + NBLK),
        out_specs=(VM, VM),
        compiler_params=params(8),
        cost_estimate=cost(1 << 31),
        name="orthonormal",
    )(gram, *blocks)


def update_body(t_ref, a_ref, b_ref, c_ref, d_ref, inv_ref, dither_ref, p3_ref, *rest):
    mem = rest[:NBLK]
    qf_ref, out_hbm, stage, sem = rest[NBLK:]
    total = (a_ref[...] + b_ref[...]) + (c_ref[...] + d_ref[...])
    qmat = jnp.dot(inv_ref[...], total, precision=HIGH, preferred_element_type=F32) / WORKERS
    scale = 1.0 + (dither_ref[...].astype(F32) / 65536.0 - 0.5) / 4.0
    qt = (qmat * scale).astype(BF16)
    qf_ref[...] = qt
    q3 = jnp.concatenate([qt, qt, qt, jnp.zeros((RANK, COLS), BF16)], axis=0)
    copies = []
    for r in range(NBLK):
        approx = jnp.dot(p3_ref[r], q3, preferred_element_type=F32)
        stage[r] = (mem[r][...] - approx).astype(BF16)
        at = pl.ds(pl.multiple_of((t_ref[0] ^ r) * COLS, COLS), COLS)
        copies.append(pltpu.make_async_copy(stage.at[r], out_hbm.at[at, :], sem.at[r]))
        copies[-1].start()
    for c in copies:
        c.wait()


def update(t, parts, inv, dither, p3, memory):
    return pl.pallas_call(
        update_body,
        out_shape=(
            jax.ShapeDtypeStruct((RANK, COLS), BF16),
            jax.ShapeDtypeStruct((D, COLS), BF16),
        ),
        in_specs=[SM] + [VM] * (len(parts) + 3 + NBLK),
        out_specs=(VM, ANY),
        scratch_shapes=[
            pltpu.VMEM((NBLK, COLS, COLS), BF16),
            pltpu.SemaphoreType.DMA((NBLK,)),
        ],
        compiler_params=params(16),
        cost_estimate=cost(2 * D * COLS * 256, 7 * MB),
        name="update",
    )(t, *parts, inv, dither, p3, *memory)


def sum_after(parts, after):
    def body(a, b, c, d, *rest):
        rest[-1][...] = (a[...] + b[...]) + (c[...] + d[...])

    return pl.pallas_call(
        body,
        out_shape=jax.ShapeDtypeStruct(parts[0].shape, F32),
        in_specs=[VM] * 4 + [ANY] * len(after),
        out_specs=VM,
        compiler_params=params(8),
        cost_estimate=cost(1000),
        name="sum_after",
    )(*parts, *after)


def swap(x, axis, size, mask):
    return lax.ppermute(x, axis, [(i, i ^ mask) for i in range(size)])


def per_device(acts, out_grad, error, q_seed, dither):
    t = lax.axis_index("tensor").astype(jnp.int32).reshape(1)

    def core(x):
        return swap(x, "tensor", NBLK, 1)

    def ring_z(x, r):
        return swap(x, "tensor", NBLK, 2 * r)

    def ring_x(x):
        return [swap(x, "dp", WORKERS, r) for r in RING]

    def ring_y(x):
        return [swap(x, "dp", WORKERS, 4 * r) for r in RING]

    away, acts_1, err_1, grad_v, t3, qt = left(1, t, acts, error, out_grad, q_seed.T)
    came = core(away)
    kept, acts_0, err_0 = left(0, t, acts, error, grad_v, None, t3, qt)
    part = kept + came
    halves = ((acts_0, err_0), (acts_1, err_1))
    from_z = [ring_z(part[r], r) for r in RING]
    even = memory_blocks((0, 1, 2), halves[0], grad_v, part)
    own = sum_after([part[0], *from_z], even[:1])

    from_x = ring_x(own)
    odd = memory_blocks((0, 1, 2), halves[1], grad_v, own)
    own = sum_after([own, *from_x], odd[:1])
    from_y = ring_y(own)
    even += memory_blocks((3,), halves[0], grad_v, own)
    odd += memory_blocks((3,), halves[1], grad_v, own)
    own = sum_after([own, *from_y], [even[3], odd[3]])

    mine, theirs = {0: own}, {0: core(own)}
    for r in RING:
        mine[r] = ring_z(own, r)
        theirs[r] = core(mine[r])
    early = right([(0, 0, mine[0]), (1, 0, theirs[0])], grad_v, halves)
    mid = right([(0, r, mine[r]) for r in RING], grad_v, halves, (early,))
    q, gram = right([(1, r, theirs[r]) for r in RING], grad_v, halves, (mid,), True)

    from_x = ring_x(q)
    p3, inv = orthonormal(gram, [b[r] for r in range(HALF) for b in (mine, theirs)])
    q = sum_after([q, *from_x], [inv])
    memory = [m[k] for k in range(HALF) for m in (even, odd)]
    q_factor, new_error = update(t, [q, *ring_y(q)], inv, dither.T, p3, memory)
    return (q_factor.T, new_error)


def solution(mesh):
    in_specs = (
        P("dp", None),
        P("dp", "tensor"),
        P("dp", "tensor"),
        P("tensor", None),
        P("tensor", None),
    )
    out_specs = (P("tensor", None), P("dp", "tensor"))
    return jax.shard_map(
        per_device, mesh=mesh, in_specs=in_specs, out_specs=out_specs, check_vma=False
    )
```

```python
import jax
import jax.numpy as jnp
from jax import lax
from jax.experimental import pallas as pl
from jax.experimental.pallas import tpu as pltpu
from jax.sharding import PartitionSpec as P

HIGH = lax.Precision.HIGHEST
F32 = jnp.float32
BF16 = jnp.bfloat16

D = 5120
TOK = 1024
COLS = 640
RANK = 32
TRI = 3 * RANK
NBLK = 8
HALF = 4
WORKERS = 16
MB = 1 << 20
RING = (1, 3, 2)
OWNER, SECOND, THIRD = "zx", "xy", "yz"
DP_FIRST, DP_SECOND = "xy", "yx"
GATHER = (0, *RING)
ORDER = tuple(2 * r + c for r in GATHER for c in (0, 1))

NT = (((1,), (1,)), ((), ()))
TN = (((0,), (0,)), ((), ()))

VM = pl.BlockSpec(memory_space=pltpu.VMEM)
SM = pl.BlockSpec(memory_space=pltpu.SMEM)
ANY = pl.BlockSpec(memory_space=pl.ANY)


def params(mb):
    return pltpu.CompilerParams(vmem_limit_bytes=mb * MB)


def cost(flops, bytes_accessed=0):
    return pl.CostEstimate(flops=flops, bytes_accessed=bytes_accessed, transcendentals=0)


def split3(x):
    hi = x.astype(BF16)
    r = x - hi.astype(F32)
    mid = r.astype(BF16)
    lo = (r - mid.astype(F32)).astype(BF16)
    return jnp.concatenate([hi, mid, lo], axis=0)


def fold3(y):
    return y[:RANK] + y[RANK : 2 * RANK] + y[2 * RANK :]


def rows_of(me, r):
    core = (me ^ r) & 1
    z, x = (me >> 1) & 3, (me >> 3) & 3
    block = ((z + core * (x - z)) ^ (r >> 1)) * 2 + core
    return pl.multiple_of(block * COLS, COLS)


def left(rs, limit, me, acts, error, grad, q_seed, t3, after):
    first = t3 is None
    n = len(rs)

    def body(me_ref, acts_hbm, err_hbm, grad_in, seed_in, *rest):
        if first:
            p_ref, acts_v, err_v, grad_v, t3_ref, qt_ref, sem, gsem, seed_v = rest
        else:
            t3_ref, p_ref, acts_v, err_v, sem = rest[:1] + rest[-4:]
            qt_ref = seed_in

        def columns(k):
            return pl.ds(rows_of(me_ref[0], rs[k]), COLS)

        acts_copy = [
            pltpu.make_async_copy(acts_hbm.at[:, columns(k)], acts_v.at[k], sem.at[0, k])
            for k in range(n)
        ]
        err_copy = [
            pltpu.make_async_copy(err_hbm.at[columns(k), :], err_v.at[k], sem.at[1, k])
            for k in range(n)
        ]
        if first:
            seed_copy = pltpu.make_async_copy(seed_in, seed_v, gsem.at[0])
            grad_copy = pltpu.make_async_copy(grad_in, grad_v, gsem.at[1])
            seed_copy.start()
            grad_copy.start()
            for k in range(n):
                err_copy[k].start()
            seed_copy.wait()
            qt_ref[...] = seed_v[...].astype(F32).astype(BF16)
            grad_copy.wait()
            acts_copy[0].start()
            tt = lax.dot_general(qt_ref[...], grad_v[...], NT, preferred_element_type=F32)
            t3_ref[...] = split3(tt)
        else:
            for k in range(n):
                err_copy[k].start()
            acts_copy[0].start()
        for k in range(n):
            err_copy[k].wait()
            if k + 1 < n:
                acts_copy[k + 1].start()
            p_ref[k] = lax.dot_general(qt_ref[...], err_v[k], NT, preferred_element_type=F32)
        for k in range(n):
            acts_copy[k].wait()
            p = fold3(jnp.dot(t3_ref[...], acts_v[k], preferred_element_type=F32))
            p_ref[k] = (p + p_ref[k]) * (1.0 / 32.0)

    out_shape = [
        jax.ShapeDtypeStruct((n, RANK, COLS), F32),
        pltpu.VMEM((n, TOK, COLS), BF16),
        pltpu.VMEM((n, COLS, COLS), BF16),
    ]
    scratch = [pltpu.SemaphoreType.DMA((2, n))]
    if first:
        out_shape += [
            pltpu.VMEM((TOK, COLS), BF16),
            pltpu.VMEM((TRI, TOK), BF16),
            pltpu.VMEM((RANK, COLS), BF16),
        ]
        scratch += [pltpu.SemaphoreType.DMA((2,)), pltpu.VMEM((RANK, COLS), jnp.int32)]
        args = (me, acts, error, grad, q_seed)
        in_specs = [SM, ANY, ANY, ANY, ANY]
    else:
        args = (me, acts, error, grad, q_seed, t3, *after)
        in_specs = [SM, ANY, ANY, VM, VM, VM] + [ANY] * len(after)
    p, acts_v, err_v, *more = pl.pallas_call(
        body,
        out_shape=out_shape,
        in_specs=in_specs,
        out_specs=[VM] * len(out_shape),
        scratch_shapes=scratch,
        compiler_params=params(limit),
        cost_estimate=cost(2 * n * 256 * COLS * (TOK + COLS), n * 2 * MB),
        name="left_first" if first else "left_more",
    )(*args)
    return p, {r: (acts_v, err_v, k) for k, r in enumerate(rs)}, more


def memory_blocks(rs, held, grad_v, after):
    n = len(rs)

    def body(*refs):
        g_ref, outs = refs[2 * n], refs[2 * n + 2 :]
        for i, r in enumerate(rs):
            a_ref, e_ref, k = refs[2 * i], refs[2 * i + 1], held[r][2]
            grad = lax.dot_general(a_ref[k], g_ref[...], TN, preferred_element_type=F32)
            outs[i][...] = grad + e_ref[k].astype(F32)

    out = pl.pallas_call(
        body,
        out_shape=[pltpu.VMEM((COLS, COLS), F32)] * n,
        in_specs=[VM] * (2 * n + 1) + [ANY],
        out_specs=[VM] * n,
        compiler_params=params(8),
        cost_estimate=cost(2 * n * COLS * COLS * TOK),
        name="memory_blocks",
    )(*(x for r in rs for x in held[r][:2]), grad_v, after)
    return dict(zip(rs, out))


def right(work, held, grad_v, earlier=None, last=False):
    n = len(work)

    def body(*refs):
        g_ref, rest = refs[3 * n], refs[3 * n + 1 :]
        given, outs = (rest[:3], rest[3:]) if earlier else ((), rest)
        tmp, q, gram = (x[...] for x in given) if earlier else (0.0, 0.0, 0.0)
        for i, (r, _, entry) in enumerate(work):
            block, a_ref, e_ref = refs[3 * i : 3 * i + 3]
            k = held[r][2]
            p = split3(block[...] if entry is None else block[entry])
            tmp = tmp + fold3(lax.dot_general(p, a_ref[k], NT, preferred_element_type=F32))
            q = q + fold3(jnp.dot(p, e_ref[k], preferred_element_type=F32))
            gram = gram + lax.dot_general(p, p, NT, preferred_element_type=F32)
        if last:
            q = q + fold3(jnp.dot(split3(tmp), g_ref[...], preferred_element_type=F32))
            outs[0][...] = q
            outs[1][...] = gram
        else:
            outs[0][...] = tmp
            outs[1][...] = q
            outs[2][...] = gram

    shapes = [
        jax.ShapeDtypeStruct((RANK, TOK), F32),
        jax.ShapeDtypeStruct((RANK, COLS), F32),
        jax.ShapeDtypeStruct((TRI, TRI), F32),
    ]
    if last:
        shapes = shapes[1:]
    args = [x for r, array, _ in work for x in (array, *held[r][:2])]
    args += [grad_v, *(earlier or ())]
    return pl.pallas_call(
        body,
        out_shape=shapes,
        in_specs=[VM] * len(args),
        out_specs=[VM] * len(shapes),
        compiler_params=params(8),
        cost_estimate=cost(2 * n * 256 * COLS * (TOK + COLS)),
        name="right_last" if last else "right_part",
    )(*args)


def orthonormal_body(gram_ref, *refs):
    mine, theirs, p3_ref, inv_ref = refs[:HALF], *refs[HALF:]
    wide = fold3(gram_ref[...])
    gram = wide[:, :RANK] + wide[:, RANK : 2 * RANK] + wide[:, 2 * RANK :]
    rows = lax.broadcasted_iota(jnp.int32, (RANK, RANK), 0)
    cols = lax.broadcasted_iota(jnp.int32, (RANK, RANK), 1)
    eye = (rows == cols).astype(F32)
    work = jnp.concatenate([gram, eye], axis=1)
    below = lax.broadcasted_iota(jnp.int32, (RANK, 1), 0)
    for k in range(RANK):
        row = work[k : k + 1, :]
        factor = jnp.where(below > k, work[:, k : k + 1] / row[:, k : k + 1], 0.0)
        work = work - factor * row
    diag = jnp.sum(work[:, :RANK] * eye, axis=1, keepdims=True)
    inv = work[:, RANK:] / jnp.sqrt(diag)
    inv_ref[...] = inv
    for k in range(NBLK):
        block = theirs[k // 2] if k % 2 else mine[k // 2][...]
        p = jnp.dot(inv, block, precision=HIGH, preferred_element_type=F32)
        hi = p.astype(BF16).astype(F32)
        r = p - hi
        mid = r.astype(BF16).astype(F32)
        stacked = jnp.concatenate([hi, mid, r - mid, jnp.zeros_like(p)], axis=0)
        p3_ref[k] = stacked.T.astype(BF16)


def orthonormal(gram, mine, theirs):
    return pl.pallas_call(
        orthonormal_body,
        out_shape=(
            pltpu.VMEM((NBLK, COLS, 4 * RANK), BF16),
            jax.ShapeDtypeStruct((RANK, RANK), F32),
        ),
        in_specs=[VM] * (2 + HALF),
        out_specs=(VM, VM),
        compiler_params=params(8),
        cost_estimate=cost(1 << 31),
        name="orthonormal",
    )(gram, *mine, theirs)


def update_body(me_ref, a_ref, b_ref, c_ref, d_ref, inv_ref, dither_ref, p3_ref, *rest):
    mem = rest[:NBLK]
    qf_ref, out_hbm, stage, sem = rest[NBLK:]
    total = (a_ref[...] + b_ref[...]) + (c_ref[...] + d_ref[...])
    qmat = jnp.dot(inv_ref[...], total, precision=HIGH, preferred_element_type=F32) / WORKERS
    scale = 1.0 + (dither_ref[...].astype(F32) / 65536.0 - 0.5) / 4.0
    qt = (qmat * scale).astype(BF16)
    qf_ref[...] = qt
    q3 = jnp.concatenate([qt, qt, qt, jnp.zeros((RANK, COLS), BF16)], axis=0)
    copies = []
    for k, r in enumerate(ORDER):
        approx = jnp.dot(p3_ref[k], q3, preferred_element_type=F32)
        stage[k] = (mem[k][...] - approx).astype(BF16)
        at = pl.ds(rows_of(me_ref[0], r), COLS)
        copies.append(pltpu.make_async_copy(stage.at[k], out_hbm.at[at, :], sem.at[k]))
        copies[-1].start()
    for c in copies:
        c.wait()


def update(me, parts, inv, dither, p3, memory):
    return pl.pallas_call(
        update_body,
        out_shape=(
            jax.ShapeDtypeStruct((RANK, COLS), BF16),
            jax.ShapeDtypeStruct((D, COLS), BF16),
        ),
        in_specs=[SM] + [VM] * (len(parts) + 3 + NBLK),
        out_specs=(VM, ANY),
        scratch_shapes=[
            pltpu.VMEM((NBLK, COLS, COLS), BF16),
            pltpu.SemaphoreType.DMA((NBLK,)),
        ],
        compiler_params=params(16),
        cost_estimate=cost(2 * D * COLS * 256, 7 * MB),
        name="update",
    )(me, *parts, inv, dither, p3, *memory)


def sum_after(parts, after):
    n = len(parts)

    def body(*refs):
        total = refs[0][...]
        for x in refs[1:n]:
            total = total + x[...]
        refs[-1][...] = total

    return pl.pallas_call(
        body,
        out_shape=jax.ShapeDtypeStruct((RANK, COLS), F32),
        in_specs=[VM] * n + [ANY] * len(after),
        out_specs=VM,
        compiler_params=params(8),
        cost_estimate=cost(1000),
        name="sum_after",
    )(*parts, *after)


def stack_after(parts, after):
    n = len(parts)

    def body(*refs):
        for i in range(n):
            refs[-1][i] = refs[i][...]

    return pl.pallas_call(
        body,
        out_shape=jax.ShapeDtypeStruct((n, RANK, COLS), F32),
        in_specs=[VM] * n + [ANY],
        out_specs=VM,
        compiler_params=params(8),
        cost_estimate=cost(1000),
        name="stack_after",
    )(*parts, after)


def place(y, x, z, core):
    return ((y * 4 + x) * 4 + z) * 2 + core


def exchange(v, axes, r):
    pairs = []
    for source in range(128):
        at = {"y": source >> 5, "x": source >> 3 & 3, "z": source >> 1 & 3}
        at[axes[source & 1]] ^= r
        pairs.append((source, place(core=source & 1, **at)))
    return lax.ppermute(v, ("dp", "tensor"), pairs)


def ring(v, axes):
    return [exchange(v, axes, r) for r in RING]


def core(v):
    return lax.ppermute(v, ("dp", "tensor"), [(i, i ^ 1) for i in range(128)])


def per_device(acts, out_grad, error, q_seed, dither):
    me = lax.axis_index(("dp", "tensor")).astype(jnp.int32).reshape(1)
    acts = pltpu.with_memory_space_constraint(acts, pltpu.HBM)
    error = pltpu.with_memory_space_constraint(error, pltpu.HBM)
    out_grad = pltpu.with_memory_space_constraint(out_grad, pltpu.HBM)
    seed = pltpu.with_memory_space_constraint(q_seed.T, pltpu.HBM)

    held = {}

    def left_of(rs, limit, grad, seed, t3, after):
        p, more_held, more = left(rs, limit, me, acts, error, grad, seed, t3, after)
        held.update(more_held)
        return p, more

    away, (grad_v, t3, qt) = left_of((1, 3, 5, 7), 8, out_grad, seed, None, ())
    came = core(away)
    kept, _ = left_of((2, 4, 6), 8, grad_v, qt, t3, ())
    part = kept + came[1:]
    from_ring = [exchange(part[r - 1], OWNER, r) for r in RING]
    kept, _ = left_of((0,), 8, grad_v, qt, t3, (part,))
    own = sum_after([kept[0], came[0], *from_ring], [])

    from_ring = ring(own, SECOND)
    memory = memory_blocks((0, 1, 2), held, grad_v, own)
    own = sum_after([own, *from_ring], [memory[0]])
    from_ring = ring(own, THIRD)
    memory |= memory_blocks((3, 4, 5), held, grad_v, own)
    own = sum_after([own, *from_ring], [memory[3]])

    mine = [own, *ring(own, OWNER)]
    early = right([(0, own, None)], held, grad_v)
    theirs = core(stack_after(mine, early[0]))
    mid = right([(2 * r, x, None) for r, x in zip(RING, mine[1:])], held, grad_v, early)
    q, gram = right([(2 * r + 1, theirs, i) for i, r in enumerate(GATHER)], held, grad_v, mid, True)

    from_ring = ring(q, DP_FIRST)
    p3, inv = orthonormal(gram, mine, theirs)
    q = sum_after([q, *from_ring], [inv])
    from_ring = ring(q, DP_SECOND)
    memory |= memory_blocks((6, 7), held, grad_v, q)
    blocks = [memory[r] for r in ORDER]
    q_factor, new_error = update(me, [q, *from_ring], inv, dither.T, p3, blocks)
    return (q_factor.T, new_error)


def solution(mesh):
    in_specs = (
        P("dp", None),
        P("dp", "tensor"),
        P("dp", "tensor"),
        P("tensor", None),
        P("tensor", None),
    )
    out_specs = (P("tensor", None), P("dp", "tensor"))
    return jax.shard_map(
        per_device, mesh=mesh, in_specs=in_specs, out_specs=out_specs, check_vma=False
    )
```

```python
import jax
import jax.numpy as jnp
from jax import lax
from jax.experimental import pallas as pl
from jax.experimental.pallas import tpu as pltpu
from jax.sharding import PartitionSpec as P

HIGH = lax.Precision.HIGHEST
F32 = jnp.float32
BF16 = jnp.bfloat16

D = 5120
TOK = 1024
COLS = 640
RANK = 32
TRI = 3 * RANK
NBLK = 8
HALF = 4
WORKERS = 16
MB = 1 << 20
RING = (1, 2, 3)
OWNER, SECOND, THIRD = "zx", "xy", "yz"
DP_FIRST, DP_SECOND = "xy", "yx"
ORDER = (0, 1, *(2 * r for r in RING), *(2 * r + 1 for r in RING))

NT = (((1,), (1,)), ((), ()))
TN = (((0,), (0,)), ((), ()))

VM = pl.BlockSpec(memory_space=pltpu.VMEM)
SM = pl.BlockSpec(memory_space=pltpu.SMEM)
ANY = pl.BlockSpec(memory_space=pl.ANY)


def params(mb):
    return pltpu.CompilerParams(vmem_limit_bytes=mb * MB)


def cost(flops, bytes_accessed=0):
    return pl.CostEstimate(flops=flops, bytes_accessed=bytes_accessed, transcendentals=0)


def split3(x):
    hi = x.astype(BF16)
    r = x - hi.astype(F32)
    mid = r.astype(BF16)
    lo = (r - mid.astype(F32)).astype(BF16)
    return jnp.concatenate([hi, mid, lo], axis=0)


def fold3(y):
    return y[:RANK] + y[RANK : 2 * RANK] + y[2 * RANK :]


def rows_of(me, r):
    core = (me ^ r) & 1
    z, x = (me >> 1) & 3, (me >> 3) & 3
    block = ((z + core * (x - z)) ^ (r >> 1)) * 2 + core
    return pl.multiple_of(block * COLS, COLS)


def left(rs, limit, me, acts, error, grad, q_seed, t3, after):
    first = t3 is None
    n = len(rs)

    def body(me_ref, acts_hbm, err_hbm, grad_in, seed_in, *rest):
        if first:
            p_ref, acts_v, err_v, grad_v, t3_ref, qt_ref, sem, gsem, seed_v = rest
        else:
            t3_ref, p_ref, acts_v, err_v, sem = rest[:1] + rest[-4:]
            qt_ref = seed_in

        def columns(k):
            return pl.ds(rows_of(me_ref[0], rs[k]), COLS)

        acts_copy = [
            pltpu.make_async_copy(acts_hbm.at[:, columns(k)], acts_v.at[k], sem.at[0, k])
            for k in range(n)
        ]
        err_copy = [
            pltpu.make_async_copy(err_hbm.at[columns(k), :], err_v.at[k], sem.at[1, k])
            for k in range(n)
        ]
        if first:
            seed_copy = pltpu.make_async_copy(seed_in, seed_v, gsem.at[0])
            grad_copy = pltpu.make_async_copy(grad_in, grad_v, gsem.at[1])
            seed_copy.start()
            grad_copy.start()
            for k in range(n):
                err_copy[k].start()
            seed_copy.wait()
            qt_ref[...] = seed_v[...].astype(F32).astype(BF16)
            grad_copy.wait()
            acts_copy[0].start()
            tt = lax.dot_general(qt_ref[...], grad_v[...], NT, preferred_element_type=F32)
            t3_ref[...] = split3(tt)
        else:
            for k in range(n):
                err_copy[k].start()
            acts_copy[0].start()
        for k in range(n):
            err_copy[k].wait()
            if k + 1 < n:
                acts_copy[k + 1].start()
            p_ref[k] = lax.dot_general(qt_ref[...], err_v[k], NT, preferred_element_type=F32)
        for k in range(n):
            acts_copy[k].wait()
            p = fold3(jnp.dot(t3_ref[...], acts_v[k], preferred_element_type=F32))
            p_ref[k] = (p + p_ref[k]) * (1.0 / 32.0)

    out_shape = [
        jax.ShapeDtypeStruct((n, RANK, COLS), F32),
        pltpu.VMEM((n, TOK, COLS), BF16),
        pltpu.VMEM((n, COLS, COLS), BF16),
    ]
    scratch = [pltpu.SemaphoreType.DMA((2, n))]
    if first:
        out_shape += [
            pltpu.VMEM((TOK, COLS), BF16),
            pltpu.VMEM((TRI, TOK), BF16),
            pltpu.VMEM((RANK, COLS), BF16),
        ]
        scratch += [pltpu.SemaphoreType.DMA((2,)), pltpu.VMEM((RANK, COLS), jnp.int32)]
        args = (me, acts, error, grad, q_seed)
        in_specs = [SM, ANY, ANY, ANY, ANY]
    else:
        args = (me, acts, error, grad, q_seed, t3, *after)
        in_specs = [SM, ANY, ANY, VM, VM, VM] + [ANY] * len(after)
    p, acts_v, err_v, *more = pl.pallas_call(
        body,
        out_shape=out_shape,
        in_specs=in_specs,
        out_specs=[VM] * len(out_shape),
        scratch_shapes=scratch,
        compiler_params=params(limit),
        cost_estimate=cost(2 * n * 256 * COLS * (TOK + COLS), n * 2 * MB),
        name="left_first" if first else "left_more",
    )(*args)
    return p, {r: (acts_v, err_v, k) for k, r in enumerate(rs)}, more


def memory_blocks(rs, held, grad_v, after):
    n = len(rs)

    def body(*refs):
        g_ref, outs = refs[2 * n], refs[2 * n + 2 :]
        for i, r in enumerate(rs):
            a_ref, e_ref, k = refs[2 * i], refs[2 * i + 1], held[r][2]
            grad = lax.dot_general(a_ref[k], g_ref[...], TN, preferred_element_type=F32)
            outs[i][...] = grad + e_ref[k].astype(F32)

    out = pl.pallas_call(
        body,
        out_shape=[pltpu.VMEM((COLS, COLS), F32)] * n,
        in_specs=[VM] * (2 * n + 1) + [ANY],
        out_specs=[VM] * n,
        compiler_params=params(8),
        cost_estimate=cost(2 * n * COLS * COLS * TOK),
        name="memory_blocks",
    )(*(x for r in rs for x in held[r][:2]), grad_v, after)
    return dict(zip(rs, out))


def right(work, held, grad_v, earlier=None, last=False):
    n = len(work)

    def body(*refs):
        g_ref, rest = refs[3 * n], refs[3 * n + 1 :]
        given, outs = (rest[:3], rest[3:]) if earlier else ((), rest)
        tmp, q, gram = (x[...] for x in given) if earlier else (0.0, 0.0, 0.0)
        for i, (r, _, entry) in enumerate(work):
            block, a_ref, e_ref = refs[3 * i : 3 * i + 3]
            k = held[r][2]
            p = split3(block[...] if entry is None else block[entry])
            tmp = tmp + fold3(lax.dot_general(p, a_ref[k], NT, preferred_element_type=F32))
            q = q + fold3(jnp.dot(p, e_ref[k], preferred_element_type=F32))
            gram = gram + lax.dot_general(p, p, NT, preferred_element_type=F32)
        if last:
            q = q + fold3(jnp.dot(split3(tmp), g_ref[...], preferred_element_type=F32))
            outs[0][...] = q
            outs[1][...] = gram
        else:
            outs[0][...] = tmp
            outs[1][...] = q
            outs[2][...] = gram

    shapes = [
        jax.ShapeDtypeStruct((RANK, TOK), F32),
        jax.ShapeDtypeStruct((RANK, COLS), F32),
        jax.ShapeDtypeStruct((TRI, TRI), F32),
    ]
    if last:
        shapes = shapes[1:]
    args = [x for r, array, _ in work for x in (array, *held[r][:2])]
    args += [grad_v, *(earlier or ())]
    return pl.pallas_call(
        body,
        out_shape=shapes,
        in_specs=[VM] * len(args),
        out_specs=[VM] * len(shapes),
        compiler_params=params(8),
        cost_estimate=cost(2 * n * 256 * COLS * (TOK + COLS)),
        name="right_last" if last else "right_part",
    )(*args)


def orthonormal_body(gram_ref, *refs):
    blocks, theirs, p3_ref, inv_ref = refs[: HALF + 1], *refs[HALF + 1 :]
    wide = fold3(gram_ref[...])
    gram = wide[:, :RANK] + wide[:, RANK : 2 * RANK] + wide[:, 2 * RANK :]
    rows = lax.broadcasted_iota(jnp.int32, (RANK, RANK), 0)
    cols = lax.broadcasted_iota(jnp.int32, (RANK, RANK), 1)
    eye = (rows == cols).astype(F32)
    work = jnp.concatenate([gram, eye], axis=1)
    wide = (RANK, 2 * RANK)
    below = lax.broadcasted_iota(jnp.int32, wide, 0)
    for k in range(0, RANK, 8):
        col = [jnp.broadcast_to(work[:, k + i : k + i + 1], wide) for i in range(8)]
        row = [work[k + i : k + i + 1, :] for i in range(8)]
        factor = []
        for i in range(8):
            f = jnp.where(below > k + i, col[i] / col[i][k + i : k + i + 1, :], 0.0)
            factor.append(f)
            for j in range(i + 1, 8):
                col[j] = col[j] - f * col[j][k + i : k + i + 1, :]
                row[j] = row[j] - f[k + j : k + j + 1, :] * row[i]
        for f, r in zip(factor, row):
            work = work - f * r
    diag = jnp.sum(work[:, :RANK] * eye, axis=1, keepdims=True)
    inv = work[:, RANK:] / jnp.sqrt(diag)
    inv_ref[...] = inv
    for k in range(NBLK):
        block = theirs[k - HALF - 1] if k > HALF else blocks[k][...]
        p = jnp.dot(inv, block, precision=HIGH, preferred_element_type=F32)
        hi = p.astype(BF16).astype(F32)
        r = p - hi
        mid = r.astype(BF16).astype(F32)
        stacked = jnp.concatenate([hi, mid, r - mid, jnp.zeros_like(p)], axis=0)
        p3_ref[k] = stacked.T.astype(BF16)


def orthonormal(gram, blocks, theirs):
    return pl.pallas_call(
        orthonormal_body,
        out_shape=(
            pltpu.VMEM((NBLK, COLS, 4 * RANK), BF16),
            jax.ShapeDtypeStruct((RANK, RANK), F32),
        ),
        in_specs=[VM] * (3 + HALF),
        out_specs=(VM, VM),
        compiler_params=params(8),
        cost_estimate=cost(1 << 31),
        name="orthonormal",
    )(gram, *blocks, theirs)


def update_body(me_ref, a_ref, b_ref, c_ref, d_ref, inv_ref, dither_ref, p3_ref, *rest):
    mem = rest[:NBLK]
    qf_ref, out_hbm, stage, sem = rest[NBLK:]
    total = (a_ref[...] + b_ref[...]) + (c_ref[...] + d_ref[...])
    qmat = jnp.dot(inv_ref[...], total, precision=HIGH, preferred_element_type=F32) / WORKERS
    scale = 1.0 + (dither_ref[...].astype(F32) / 65536.0 - 0.5) / 4.0
    qt = (qmat * scale).astype(BF16)
    qf_ref[...] = qt
    q3 = jnp.concatenate([qt, qt, qt, jnp.zeros((RANK, COLS), BF16)], axis=0)
    copies = []
    for k, r in enumerate(ORDER):
        approx = jnp.dot(p3_ref[k], q3, preferred_element_type=F32)
        stage[k] = (mem[k][...] - approx).astype(BF16)
        at = pl.ds(rows_of(me_ref[0], r), COLS)
        copies.append(pltpu.make_async_copy(stage.at[k], out_hbm.at[at, :], sem.at[k]))
        copies[-1].start()
    for c in copies:
        c.wait()


def update(me, parts, inv, dither, p3, memory):
    return pl.pallas_call(
        update_body,
        out_shape=(
            jax.ShapeDtypeStruct((RANK, COLS), BF16),
            jax.ShapeDtypeStruct((D, COLS), BF16),
        ),
        in_specs=[SM] + [VM] * (len(parts) + 3 + NBLK),
        out_specs=(VM, ANY),
        scratch_shapes=[
            pltpu.VMEM((NBLK, COLS, COLS), BF16),
            pltpu.SemaphoreType.DMA((NBLK,)),
        ],
        compiler_params=params(16),
        cost_estimate=cost(2 * D * COLS * 256, 7 * MB),
        name="update",
    )(me, *parts, inv, dither, p3, *memory)


def sum_after(parts, after):
    n = len(parts)

    def body(*refs):
        total = refs[0][...]
        for x in refs[1:n]:
            total = total + x[...]
        refs[-1][...] = total

    return pl.pallas_call(
        body,
        out_shape=jax.ShapeDtypeStruct((RANK, COLS), F32),
        in_specs=[VM] * n + [ANY] * len(after),
        out_specs=VM,
        compiler_params=params(8),
        cost_estimate=cost(1000),
        name="sum_after",
    )(*parts, *after)


def stack_after(parts, after):
    n = len(parts)

    def body(*refs):
        for i in range(n):
            refs[-1][i] = refs[i][...]

    return pl.pallas_call(
        body,
        out_shape=jax.ShapeDtypeStruct((n, RANK, COLS), F32),
        in_specs=[VM] * n + [ANY] * len(after),
        out_specs=VM,
        compiler_params=params(8),
        cost_estimate=cost(1000),
        name="stack_after",
    )(*parts, *after)


def place(y, x, z, core):
    return ((y * 4 + x) * 4 + z) * 2 + core


def exchange(v, axes, r):
    pairs = []
    for source in range(128):
        at = {"y": source >> 5, "x": source >> 3 & 3, "z": source >> 1 & 3}
        at[axes[source & 1]] ^= r
        pairs.append((source, place(core=source & 1, **at)))
    return lax.ppermute(v, ("dp", "tensor"), pairs)


def ring(v, axes):
    return [exchange(v, axes, r) for r in RING]


def core(v):
    return lax.ppermute(v, ("dp", "tensor"), [(i, i ^ 1) for i in range(128)])


def per_device(acts, out_grad, error, q_seed, dither):
    me = lax.axis_index(("dp", "tensor")).astype(jnp.int32).reshape(1)
    acts = pltpu.with_memory_space_constraint(acts, pltpu.HBM)
    error = pltpu.with_memory_space_constraint(error, pltpu.HBM)
    out_grad = pltpu.with_memory_space_constraint(out_grad, pltpu.HBM)
    seed = pltpu.with_memory_space_constraint(q_seed.T, pltpu.HBM)

    held = {}

    def left_of(rs, limit, grad, seed, t3, after):
        p, more_held, more = left(rs, limit, me, acts, error, grad, seed, t3, after)
        held.update(more_held)
        return p, more

    away, (grad_v, t3, qt) = left_of((1, 3, 5, 7), 8, out_grad, seed, None, ())
    came = core(away)
    kept, _ = left_of((2, 4, 6), 8, grad_v, qt, t3, ())
    part = kept + came[1:]
    from_ring = [exchange(part[r - 1], OWNER, r) for r in RING]
    kept, _ = left_of((0,), 8, grad_v, qt, t3, (part,))
    memory = memory_blocks((2,), held, grad_v, part)
    own = sum_after([kept[0], came[0], *from_ring], [memory[2]])

    from_ring = ring(own, SECOND)
    memory |= memory_blocks((0, 3), held, grad_v, own)
    own = sum_after([own, *from_ring], [memory[0]])
    from_ring = ring(own, THIRD)
    memory |= memory_blocks((1, 4), held, grad_v, own)
    own = sum_after([own, *from_ring], [memory[1]])

    other = core(own)
    mine = ring(own, OWNER)
    memory |= memory_blocks((5,), held, grad_v, own)
    early = right([(0, own, None), (1, other, None)], held, grad_v)
    theirs = core(stack_after(mine, [early[0], memory[5]]))
    mid = right([(2 * r, x, None) for r, x in zip(RING, mine)], held, grad_v, early)
    q, gram = right([(2 * r + 1, theirs, i) for i, r in enumerate(RING)], held, grad_v, mid, True)

    from_ring = ring(q, DP_FIRST)
    p3, inv = orthonormal(gram, [own, other, *mine], theirs)
    memory |= memory_blocks((6,), held, grad_v, q)
    q = sum_after([q, *from_ring], [inv, memory[6]])
    from_ring = ring(q, DP_SECOND)
    memory |= memory_blocks((7,), held, grad_v, q)
    q_factor, new_error = update(me, [q, *from_ring], inv, dither.T, p3, [memory[r] for r in ORDER])
    return (q_factor.T, new_error)


def solution(mesh):
    in_specs = (
        P("dp", None),
        P("dp", "tensor"),
        P("dp", "tensor"),
        P("tensor", None),
        P("tensor", None),
    )
    out_specs = (P("tensor", None), P("dp", "tensor"))
    return jax.shard_map(
        per_device, mesh=mesh, in_specs=in_specs, out_specs=out_specs, check_vma=False
    )
```

```python
import jax
import jax.numpy as jnp
from jax import lax
from jax.experimental import pallas as pl
from jax.experimental.pallas import tpu as pltpu
from jax.sharding import PartitionSpec as P

HIGH = lax.Precision.HIGHEST
F32 = jnp.float32
BF16 = jnp.bfloat16

D = 5120
TOK = 1024
COLS = 640
RANK = 32
TRI = 3 * RANK
NBLK = 8
HALF = 4
WORKERS = 16
MB = 1 << 20
RING = (1, 2, 3)
OWNER, SECOND, THIRD = "xz", "yx", "zy"
DP_FIRST, DP_SECOND = "xy", "yx"
ORDER = (0, 1, *(2 * r for r in RING), *(2 * r + 1 for r in RING))

NT = (((1,), (1,)), ((), ()))
TN = (((0,), (0,)), ((), ()))

VM = pl.BlockSpec(memory_space=pltpu.VMEM)
SM = pl.BlockSpec(memory_space=pltpu.SMEM)
ANY = pl.BlockSpec(memory_space=pl.ANY)


def params(mb):
    return pltpu.CompilerParams(vmem_limit_bytes=mb * MB)


def cost(flops, bytes_accessed=0):
    return pl.CostEstimate(flops=flops, bytes_accessed=bytes_accessed, transcendentals=0)


def split3(x):
    hi = x.astype(BF16)
    r = x - hi.astype(F32)
    mid = r.astype(BF16)
    lo = (r - mid.astype(F32)).astype(BF16)
    return jnp.concatenate([hi, mid, lo], axis=0)


def fold3(y):
    return y[:RANK] + y[RANK : 2 * RANK] + y[2 * RANK :]


def rows_of(me, r):
    core = (me ^ r) & 1
    z, x = (me >> 1) & 3, (me >> 3) & 3
    block = ((x + core * (z - x)) ^ (r >> 1)) * 2 + core
    return pl.multiple_of(block * COLS, COLS)


def copies_in(me_ref, rs, acts_hbm, acts_v, sem):
    return [
        pltpu.make_async_copy(
            acts_hbm.at[:, pl.ds(rows_of(me_ref[0], r), COLS)], acts_v.at[k], sem.at[k]
        )
        for k, r in enumerate(rs)
    ]


def copies_in_rows(me_ref, rs, err_hbm, err_v, sem):
    return [
        pltpu.make_async_copy(
            err_hbm.at[pl.ds(rows_of(me_ref[0], r), COLS), :], err_v.at[k], sem.at[k]
        )
        for k, r in enumerate(rs)
    ]


def left_away(me, error, out_grad, seed):
    rs = (1, 3, 5, 7)

    def body(me_ref, err_hbm, grad_hbm, seed_hbm, away, err_v, grad_v, qt_ref, sem, more, seed_v):
        seed_copy = pltpu.make_async_copy(seed_hbm, seed_v, more.at[0])
        grad_copy = pltpu.make_async_copy(grad_hbm, grad_v, more.at[1])
        err_copy = copies_in_rows(me_ref, rs, err_hbm, err_v, sem)
        seed_copy.start()
        err_copy[0].start()
        err_copy[1].start()
        grad_copy.start()
        seed_copy.wait()
        qt = seed_v[...].astype(F32).astype(BF16)
        qt_ref[...] = qt

        def multiply(k):
            err_copy[k].wait()
            if k + 2 < HALF:
                err_copy[k + 2].start()
            away[:, k * COLS : (k + 1) * COLS] = lax.dot_general(
                qt, err_v[k], NT, preferred_element_type=F32
            )

        multiply(0)
        multiply(1)
        grad_copy.wait()
        away[:, HALF * COLS :] = lax.dot_general(
            qt, grad_v[...], NT, preferred_element_type=F32
        )
        multiply(2)
        multiply(3)

    away, err_v, grad_v, qt = pl.pallas_call(
        body,
        out_shape=[
            jax.ShapeDtypeStruct((RANK, HALF * COLS + TOK), F32),
            pltpu.VMEM((HALF, COLS, COLS), BF16),
            pltpu.VMEM((TOK, COLS), BF16),
            pltpu.VMEM((RANK, COLS), BF16),
        ],
        in_specs=[SM, ANY, ANY, ANY],
        out_specs=[VM] * 4,
        scratch_shapes=[
            pltpu.SemaphoreType.DMA((HALF,)),
            pltpu.SemaphoreType.DMA((2,)),
            pltpu.VMEM((RANK, COLS), jnp.int32),
        ],
        compiler_params=params(8),
        cost_estimate=cost(2 * HALF * 256 * COLS * COLS, 5 * MB),
        name="left_away",
    )(me, error, out_grad, seed)
    return away, {r: (err_v, k) for k, r in enumerate(rs)}, grad_v, qt


def left_kept(me, acts, error, qt):
    rs = (2, 4, 6)

    def body(me_ref, acts_hbm, err_hbm, qt_ref, kept, acts_v, err_v, sem, acts_sem):
        err_copy = copies_in_rows(me_ref, rs, err_hbm, err_v, sem)
        acts_copy = copies_in(me_ref, rs[:1], acts_hbm, acts_v, acts_sem)
        for c in err_copy + acts_copy:
            c.start()
        for k, c in enumerate(err_copy):
            c.wait()
            kept[k] = lax.dot_general(qt_ref[...], err_v[k], NT, preferred_element_type=F32)
        for c in acts_copy:
            c.wait()

    kept, acts_v, err_v = pl.pallas_call(
        body,
        out_shape=[
            jax.ShapeDtypeStruct((3, RANK, COLS), F32),
            pltpu.VMEM((1, TOK, COLS), BF16),
            pltpu.VMEM((3, COLS, COLS), BF16),
        ],
        in_specs=[SM, ANY, ANY, VM],
        out_specs=[VM] * 3,
        scratch_shapes=[pltpu.SemaphoreType.DMA((3,)), pltpu.SemaphoreType.DMA((1,))],
        compiler_params=params(8),
        cost_estimate=cost(2 * 3 * 256 * COLS * COLS, 4 * MB),
        name="left_kept",
    )(me, acts, error, qt)
    return kept, {2: (acts_v, 0)}, {r: (err_v, k) for k, r in enumerate(rs)}


def left_sum(me, acts, acts_2, kept, away, came):
    rs = (4, 6)

    def body(me_ref, acts_hbm, first, kept, away, came, part, acts_v, t3_ref, sem):
        acts_copy = copies_in(me_ref, rs, acts_hbm, acts_v, sem)
        for c in acts_copy:
            c.start()
        t3_ref[...] = split3(away[:, HALF * COLS :] + came[:, HALF * COLS :])
        for k in range(3):
            if k:
                acts_copy[k - 1].wait()
            block = acts_v[k - 1] if k else first[0]
            p = fold3(jnp.dot(t3_ref[...], block, preferred_element_type=F32))
            p = p + (kept[k] + came[:, (k + 1) * COLS : (k + 2) * COLS])
            part[k] = p * (1.0 / 32.0)

    part, acts_v, t3 = pl.pallas_call(
        body,
        out_shape=[
            jax.ShapeDtypeStruct((3, RANK, COLS), F32),
            pltpu.VMEM((2, TOK, COLS), BF16),
            pltpu.VMEM((TRI, TOK), BF16),
        ],
        in_specs=[SM, ANY] + [VM] * 4,
        out_specs=[VM] * 3,
        scratch_shapes=[pltpu.SemaphoreType.DMA((2,))],
        compiler_params=params(8),
        cost_estimate=cost(2 * 3 * 256 * COLS * TOK, 3 * MB),
        name="left_sum",
    )(me, acts, acts_2, kept, away, came)
    return part, {r: (acts_v, k) for k, r in enumerate(rs)}, t3


def left_own(me, acts, error, qt, t3, came, after):
    def body(me_ref, acts_hbm, err_hbm, qt_ref, t3_ref, came, after_ref, p0, acts_v, err_v, sem):
        err_copy = copies_in_rows(me_ref, (0,), err_hbm, err_v, sem.at[0])
        acts_copy = copies_in(me_ref, (0,), acts_hbm, acts_v, sem.at[1])
        err_copy[0].start()
        acts_copy[0].start()
        err_copy[0].wait()
        p = lax.dot_general(qt_ref[...], err_v[0], NT, preferred_element_type=F32)
        p = p + came[:, :COLS]
        acts_copy[0].wait()
        p = p + fold3(jnp.dot(t3_ref[...], acts_v[0], preferred_element_type=F32))
        p0[...] = p * (1.0 / 32.0)

    p0, acts_v, err_v = pl.pallas_call(
        body,
        out_shape=[
            jax.ShapeDtypeStruct((RANK, COLS), F32),
            pltpu.VMEM((1, TOK, COLS), BF16),
            pltpu.VMEM((1, COLS, COLS), BF16),
        ],
        in_specs=[SM, ANY, ANY, VM, VM, VM, ANY],
        out_specs=[VM] * 3,
        scratch_shapes=[pltpu.SemaphoreType.DMA((2, 1))],
        compiler_params=params(8),
        cost_estimate=cost(2 * 256 * COLS * (TOK + COLS), 2 * MB),
        name="left_own",
    )(me, acts, error, qt, t3, came, after)
    return p0, {0: (acts_v, 0)}, {0: (err_v, 0)}


def memory_blocks(rs, held_a, held_e, grad_v, after, load=(), me=None, acts=None):
    n, m = len(rs), len(load)

    def body(*refs):
        g_ref, rest = refs[2 * n], refs[2 * n + 2 :]
        copies = []
        if m:
            me_ref, acts_hbm, sem = rest[0], rest[1], rest[-1]
            rest = rest[2:-1]
            copies = copies_in(me_ref, load, acts_hbm, rest[n], sem)
        for c in copies:
            c.start()
        for i, r in enumerate(rs):
            a_ref, e_ref = refs[2 * i : 2 * i + 2]
            grad = lax.dot_general(
                a_ref[held_a[r][1]], g_ref[...], TN, preferred_element_type=F32
            )
            rest[i][...] = grad + e_ref[held_e[r][1]].astype(F32)
        for c in copies:
            c.wait()

    shapes = [pltpu.VMEM((COLS, COLS), F32)] * n
    args = [x for r in rs for x in (held_a[r][0], held_e[r][0])] + [grad_v, after]
    in_specs = [VM] * (2 * n + 1) + [ANY]
    if m:
        shapes.append(pltpu.VMEM((m, TOK, COLS), BF16))
        args += [me, acts]
        in_specs += [SM, ANY]
    out = pl.pallas_call(
        body,
        out_shape=shapes,
        in_specs=in_specs,
        out_specs=[VM] * len(shapes),
        scratch_shapes=[pltpu.SemaphoreType.DMA((m,))] if m else [],
        compiler_params=params(8),
        cost_estimate=cost(2 * n * COLS * COLS * TOK),
        name="memory_blocks",
    )(*args)
    return dict(zip(rs, out)), {r: (out[n], k) for k, r in enumerate(load)}


def right(work, held_a, held_e, grad_v, earlier=None, last=False):
    n = len(work)

    def body(*refs):
        g_ref, rest = refs[3 * n], refs[3 * n + 1 :]
        given, outs = (rest[:3], rest[3:]) if earlier else ((), rest)
        tmp, q, gram = (x[...] for x in given) if earlier else (0.0, 0.0, 0.0)
        for i, (r, _, entry) in enumerate(work):
            block, a_ref, e_ref = refs[3 * i : 3 * i + 3]
            a, e = a_ref[held_a[r][1]], e_ref[held_e[r][1]]
            p = split3(block[...] if entry is None else block[entry])
            tmp = tmp + fold3(lax.dot_general(p, a, NT, preferred_element_type=F32))
            q = q + fold3(jnp.dot(p, e, preferred_element_type=F32))
            gram = gram + lax.dot_general(p, p, NT, preferred_element_type=F32)
        if last:
            q = q + fold3(jnp.dot(split3(tmp), g_ref[...], preferred_element_type=F32))
            outs[0][...] = q
            outs[1][...] = gram
        else:
            outs[0][...] = tmp
            outs[1][...] = q
            outs[2][...] = gram

    shapes = [
        jax.ShapeDtypeStruct((RANK, TOK), F32),
        jax.ShapeDtypeStruct((RANK, COLS), F32),
        jax.ShapeDtypeStruct((TRI, TRI), F32),
    ]
    if last:
        shapes = shapes[1:]
    args = [x for r, array, _ in work for x in (array, held_a[r][0], held_e[r][0])]
    args += [grad_v, *(earlier or ())]
    return pl.pallas_call(
        body,
        out_shape=shapes,
        in_specs=[VM] * len(args),
        out_specs=[VM] * len(shapes),
        compiler_params=params(8),
        cost_estimate=cost(2 * n * 256 * COLS * (TOK + COLS)),
        name="right_last" if last else "right_part",
    )(*args)


def orthonormal_body(gram_ref, *refs):
    blocks, theirs, p3_ref, inv_ref = refs[: HALF + 1], *refs[HALF + 1 :]
    wide = fold3(gram_ref[...])
    gram = wide[:, :RANK] + wide[:, RANK : 2 * RANK] + wide[:, 2 * RANK :]
    rows = lax.broadcasted_iota(jnp.int32, (RANK, RANK), 0)
    cols = lax.broadcasted_iota(jnp.int32, (RANK, RANK), 1)
    eye = (rows == cols).astype(F32)
    work = jnp.concatenate([gram, eye], axis=1)
    wide = (RANK, 2 * RANK)
    below = lax.broadcasted_iota(jnp.int32, wide, 0)
    for k in range(0, RANK, 8):
        col = [jnp.broadcast_to(work[:, k + i : k + i + 1], wide) for i in range(8)]
        row = [work[k + i : k + i + 1, :] for i in range(8)]
        factor = []
        for i in range(8):
            f = jnp.where(below > k + i, col[i] / col[i][k + i : k + i + 1, :], 0.0)
            factor.append(f)
            for j in range(i + 1, 8):
                col[j] = col[j] - f * col[j][k + i : k + i + 1, :]
                row[j] = row[j] - f[k + j : k + j + 1, :] * row[i]
        for f, r in zip(factor, row):
            work = work - f * r
    diag = jnp.sum(work[:, :RANK] * eye, axis=1, keepdims=True)
    inv = work[:, RANK:] / jnp.sqrt(diag)
    inv_ref[...] = inv
    for k in range(NBLK):
        block = theirs[k - HALF - 1] if k > HALF else blocks[k][...]
        p = jnp.dot(inv, block, precision=HIGH, preferred_element_type=F32)
        hi = p.astype(BF16).astype(F32)
        r = p - hi
        mid = r.astype(BF16).astype(F32)
        stacked = jnp.concatenate([hi, mid, r - mid, jnp.zeros_like(p)], axis=0)
        p3_ref[k] = stacked.T.astype(BF16)


def orthonormal(gram, blocks, theirs):
    return pl.pallas_call(
        orthonormal_body,
        out_shape=(
            pltpu.VMEM((NBLK, COLS, 4 * RANK), BF16),
            jax.ShapeDtypeStruct((RANK, RANK), F32),
        ),
        in_specs=[VM] * (3 + HALF),
        out_specs=(VM, VM),
        compiler_params=params(8),
        cost_estimate=cost(1 << 31),
        name="orthonormal",
    )(gram, *blocks, theirs)


def update_body(me_ref, a_ref, b_ref, c_ref, d_ref, inv_ref, dither_ref, p3_ref, *rest):
    mem = rest[:NBLK]
    qf_ref, out_hbm, stage, sem = rest[NBLK:]
    total = (a_ref[...] + b_ref[...]) + (c_ref[...] + d_ref[...])
    qmat = jnp.dot(inv_ref[...], total, precision=HIGH, preferred_element_type=F32) / WORKERS
    scale = 1.0 + (dither_ref[...].astype(F32) / 65536.0 - 0.5) / 4.0
    qt = (qmat * scale).astype(BF16)
    qf_ref[...] = qt
    q3 = jnp.concatenate([qt, qt, qt, jnp.zeros((RANK, COLS), BF16)], axis=0)
    copies = []
    for k, r in enumerate(ORDER):
        approx = jnp.dot(p3_ref[k], q3, preferred_element_type=F32)
        stage[k] = (mem[k][...] - approx).astype(BF16)
        at = pl.ds(rows_of(me_ref[0], r), COLS)
        copies.append(pltpu.make_async_copy(stage.at[k], out_hbm.at[at, :], sem.at[k]))
        copies[-1].start()
    for c in copies:
        c.wait()


def update(me, parts, inv, dither, p3, memory):
    return pl.pallas_call(
        update_body,
        out_shape=(
            jax.ShapeDtypeStruct((RANK, COLS), BF16),
            jax.ShapeDtypeStruct((D, COLS), BF16),
        ),
        in_specs=[SM] + [VM] * (len(parts) + 3 + NBLK),
        out_specs=(VM, ANY),
        scratch_shapes=[
            pltpu.VMEM((NBLK, COLS, COLS), BF16),
            pltpu.SemaphoreType.DMA((NBLK,)),
        ],
        compiler_params=params(16),
        cost_estimate=cost(2 * D * COLS * 256, 7 * MB),
        name="update",
    )(me, *parts, inv, dither, p3, *memory)


def sum_after(parts, after):
    n = len(parts)

    def body(*refs):
        total = refs[0][...]
        for x in refs[1:n]:
            total = total + x[...]
        refs[-1][...] = total

    return pl.pallas_call(
        body,
        out_shape=jax.ShapeDtypeStruct((RANK, COLS), F32),
        in_specs=[VM] * n + [ANY] * len(after),
        out_specs=VM,
        compiler_params=params(8),
        cost_estimate=cost(1000),
        name="sum_after",
    )(*parts, *after)


def stack_after(parts, after):
    n = len(parts)

    def body(*refs):
        for i in range(n):
            refs[-1][i] = refs[i][...]

    return pl.pallas_call(
        body,
        out_shape=jax.ShapeDtypeStruct((n, RANK, COLS), F32),
        in_specs=[VM] * n + [ANY] * len(after),
        out_specs=VM,
        compiler_params=params(8),
        cost_estimate=cost(1000),
        name="stack_after",
    )(*parts, *after)


def place(y, x, z, core):
    return ((y * 4 + x) * 4 + z) * 2 + core


def exchange(v, axes, r):
    pairs = []
    for source in range(128):
        at = {"y": source >> 5, "x": source >> 3 & 3, "z": source >> 1 & 3}
        at[axes[source & 1]] ^= r
        pairs.append((source, place(core=source & 1, **at)))
    return lax.ppermute(v, ("dp", "tensor"), pairs)


def ring(v, axes):
    return [exchange(v, axes, r) for r in RING]


def core(v):
    return lax.ppermute(v, ("dp", "tensor"), [(i, i ^ 1) for i in range(128)])


def per_device(acts, out_grad, error, q_seed, dither):
    me = lax.axis_index(("dp", "tensor")).astype(jnp.int32).reshape(1)
    acts = pltpu.with_memory_space_constraint(acts, pltpu.HBM)
    error = pltpu.with_memory_space_constraint(error, pltpu.HBM)
    out_grad = pltpu.with_memory_space_constraint(out_grad, pltpu.HBM)
    seed = pltpu.with_memory_space_constraint(q_seed.T, pltpu.HBM)

    away, held_e, grad_v, qt = left_away(me, error, out_grad, seed)
    came = core(away)
    kept, held_a, more_e = left_kept(me, acts, error, qt)
    held_e |= more_e
    part, more_a, t3 = left_sum(me, acts, held_a[2][0], kept, away, came)
    held_a |= more_a
    from_ring = [exchange(part[r - 1], OWNER, r) for r in RING]
    own, more_a, more_e = left_own(me, acts, error, qt, t3, came, part)
    held_a |= more_a
    held_e |= more_e
    memory = {}

    def memory_of(rs, after, load=()):
        blocks, more = memory_blocks(rs, held_a, held_e, grad_v, after, load, me, acts)
        memory.update(blocks)
        held_a.update(more)

    memory_of((2,), part)
    own = sum_after([own, *from_ring], [memory[2]])

    from_ring = ring(own, SECOND)
    memory_of((0,), own, (1, 3))
    own = sum_after([own, *from_ring], [memory[0]])
    from_ring = ring(own, THIRD)
    memory_of((4,), own, (5, 7))
    own = sum_after([own, *from_ring], [memory[4]])

    other = core(own)
    mine = ring(own, OWNER)
    memory_of((1,), own)
    held = (held_a, held_e, grad_v)
    early = right([(0, own, None), (1, other, None)], *held)
    early = right([(2 * RING[2], mine[2], None)], *held, early)
    theirs = core(stack_after(mine, [early[0], memory[1]]))
    mid = right([(2 * r, x, None) for r, x in zip(RING[:2], mine)], *held, early)
    q, gram = right([(2 * r + 1, theirs, i) for i, r in enumerate(RING)], *held, mid, True)

    from_ring = ring(q, DP_FIRST)
    p3, inv = orthonormal(gram, [own, other, *mine], theirs)
    memory_of((3,), q)
    q = sum_after([q, *from_ring], [inv, memory[3]])
    from_ring = ring(q, DP_SECOND)
    memory_of((5, 6, 7), q)
    q_factor, new_error = update(me, [q, *from_ring], inv, dither.T, p3, [memory[r] for r in ORDER])
    return (q_factor.T, new_error)


def solution(mesh):
    in_specs = (
        P("dp", None),
        P("dp", "tensor"),
        P("dp", "tensor"),
        P("tensor", None),
        P("tensor", None),
    )
    out_specs = (P("tensor", None), P("dp", "tensor"))
    return jax.shard_map(
        per_device, mesh=mesh, in_specs=in_specs, out_specs=out_specs, check_vma=False
    )
```

```python
import jax
import jax.numpy as jnp
from jax import lax
from jax.experimental import pallas as pl
from jax.experimental.pallas import tpu as pltpu
from jax.sharding import PartitionSpec as P

HIGH = lax.Precision.HIGHEST
F32 = jnp.float32
BF16 = jnp.bfloat16

D = 5120
TOK = 1024
COLS = 640
RANK = 32
TRI = 3 * RANK
NBLK = 8
HALF = 4
WORKERS = 16
MB = 1 << 20
RING = (1, 2, 3)
OWNER, SECOND, THIRD = "xz", "yx", "zy"
DP_FIRST, DP_SECOND = "xy", "yx"
ORDER = (0, 1, *(2 * r for r in RING), *(2 * r + 1 for r in RING))

NT = (((1,), (1,)), ((), ()))
TN = (((0,), (0,)), ((), ()))

VM = pl.BlockSpec(memory_space=pltpu.VMEM)
SM = pl.BlockSpec(memory_space=pltpu.SMEM)
ANY = pl.BlockSpec(memory_space=pl.ANY)


def params(mb):
    return pltpu.CompilerParams(vmem_limit_bytes=mb * MB)


def cost(flops, bytes_accessed=0):
    return pl.CostEstimate(flops=flops, bytes_accessed=bytes_accessed, transcendentals=0)


def split3(x):
    hi = x.astype(BF16)
    r = x - hi.astype(F32)
    mid = r.astype(BF16)
    lo = (r - mid.astype(F32)).astype(BF16)
    return jnp.concatenate([hi, mid, lo], axis=0)


def fold3(y):
    return y[:RANK] + y[RANK : 2 * RANK] + y[2 * RANK :]


def rows_of(me, r):
    core = (me ^ r) & 1
    z, x = (me >> 1) & 3, (me >> 3) & 3
    block = ((x + core * (z - x)) ^ (r >> 1)) * 2 + core
    return pl.multiple_of(block * COLS, COLS)


def copies_in(me_ref, rs, acts_hbm, acts_v, sem):
    return [
        pltpu.make_async_copy(
            acts_hbm.at[:, pl.ds(rows_of(me_ref[0], r), COLS)], acts_v.at[k], sem.at[k]
        )
        for k, r in enumerate(rs)
    ]


def copies_in_rows(me_ref, rs, err_hbm, err_v, sem):
    return [
        pltpu.make_async_copy(
            err_hbm.at[pl.ds(rows_of(me_ref[0], r), COLS), :], err_v.at[k], sem.at[k]
        )
        for k, r in enumerate(rs)
    ]


def left_away(me, error, out_grad, seed):
    rs = (1, 3, 5, 7)

    def body(me_ref, err_hbm, grad_hbm, seed_hbm, away, err_v, grad_v, qt_ref, sem, more, seed_v):
        seed_copy = pltpu.make_async_copy(seed_hbm, seed_v, more.at[0])
        grad_copy = pltpu.make_async_copy(grad_hbm, grad_v, more.at[1])
        err_copy = copies_in_rows(me_ref, rs, err_hbm, err_v, sem)
        seed_copy.start()
        err_copy[0].start()
        err_copy[1].start()
        grad_copy.start()
        seed_copy.wait()
        qt = seed_v[...].astype(F32).astype(BF16)
        qt_ref[...] = qt

        def multiply(k):
            err_copy[k].wait()
            if k + 2 < HALF:
                err_copy[k + 2].start()
            away[:, k * COLS : (k + 1) * COLS] = lax.dot_general(
                qt, err_v[k], NT, preferred_element_type=F32
            )

        multiply(0)
        multiply(1)
        grad_copy.wait()
        away[:, HALF * COLS :] = lax.dot_general(
            qt, grad_v[...], NT, preferred_element_type=F32
        )
        multiply(2)
        multiply(3)

    away, err_v, grad_v, qt = pl.pallas_call(
        body,
        out_shape=[
            jax.ShapeDtypeStruct((RANK, HALF * COLS + TOK), F32),
            pltpu.VMEM((HALF, COLS, COLS), BF16),
            pltpu.VMEM((TOK, COLS), BF16),
            pltpu.VMEM((RANK, COLS), BF16),
        ],
        in_specs=[SM, ANY, ANY, ANY],
        out_specs=[VM] * 4,
        scratch_shapes=[
            pltpu.SemaphoreType.DMA((HALF,)),
            pltpu.SemaphoreType.DMA((2,)),
            pltpu.VMEM((RANK, COLS), jnp.int32),
        ],
        compiler_params=params(8),
        cost_estimate=cost(2 * HALF * 256 * COLS * COLS, 5 * MB),
        name="left_away",
    )(me, error, out_grad, seed)
    return away, {r: (err_v, k) for k, r in enumerate(rs)}, grad_v, qt


def left_kept(me, acts, error, qt):
    rs = (2, 4, 6)

    def body(me_ref, acts_hbm, err_hbm, qt_ref, kept, acts_v, err_v, sem, acts_sem):
        err_copy = copies_in_rows(me_ref, rs, err_hbm, err_v, sem)
        acts_copy = copies_in(me_ref, rs, acts_hbm, acts_v, acts_sem)
        for c in err_copy + acts_copy:
            c.start()
        for k, c in enumerate(err_copy):
            c.wait()
            kept[k] = lax.dot_general(qt_ref[...], err_v[k], NT, preferred_element_type=F32)
        for c in acts_copy:
            c.wait()

    kept, acts_v, err_v = pl.pallas_call(
        body,
        out_shape=[
            jax.ShapeDtypeStruct((3, RANK, COLS), F32),
            pltpu.VMEM((3, TOK, COLS), BF16),
            pltpu.VMEM((3, COLS, COLS), BF16),
        ],
        in_specs=[SM, ANY, ANY, VM],
        out_specs=[VM] * 3,
        scratch_shapes=[pltpu.SemaphoreType.DMA((3,)), pltpu.SemaphoreType.DMA((3,))],
        compiler_params=params(8),
        cost_estimate=cost(2 * 3 * 256 * COLS * COLS, 6 * MB),
        name="left_kept",
    )(me, acts, error, qt)
    return kept, {r: (acts_v, k) for k, r in enumerate(rs)}, {r: (err_v, k) for k, r in enumerate(rs)}


def left_sum(acts_v, kept, away, came):
    def body(acts_v, kept, away, came, part, t3_ref):
        t3_ref[...] = split3(away[:, HALF * COLS :] + came[:, HALF * COLS :])
        for k in range(3):
            p = fold3(jnp.dot(t3_ref[...], acts_v[k], preferred_element_type=F32))
            p = p + (kept[k] + came[:, (k + 1) * COLS : (k + 2) * COLS])
            part[k] = p * (1.0 / 32.0)

    return pl.pallas_call(
        body,
        out_shape=[
            jax.ShapeDtypeStruct((3, RANK, COLS), F32),
            pltpu.VMEM((TRI, TOK), BF16),
        ],
        in_specs=[VM] * 4,
        out_specs=[VM] * 2,
        compiler_params=params(8),
        cost_estimate=cost(2 * 3 * 256 * COLS * TOK),
        name="left_sum",
    )(acts_v, kept, away, came)


def left_own(me, acts, error, qt, t3, came, after):
    def body(me_ref, acts_hbm, err_hbm, qt_ref, t3_ref, came, after_ref, p0, acts_v, err_v, sem):
        err_copy = copies_in_rows(me_ref, (0,), err_hbm, err_v, sem.at[0])
        acts_copy = copies_in(me_ref, (0,), acts_hbm, acts_v, sem.at[1])
        err_copy[0].start()
        acts_copy[0].start()
        err_copy[0].wait()
        p = lax.dot_general(qt_ref[...], err_v[0], NT, preferred_element_type=F32)
        p = p + came[:, :COLS]
        acts_copy[0].wait()
        p = p + fold3(jnp.dot(t3_ref[...], acts_v[0], preferred_element_type=F32))
        p0[...] = p * (1.0 / 32.0)

    p0, acts_v, err_v = pl.pallas_call(
        body,
        out_shape=[
            jax.ShapeDtypeStruct((RANK, COLS), F32),
            pltpu.VMEM((1, TOK, COLS), BF16),
            pltpu.VMEM((1, COLS, COLS), BF16),
        ],
        in_specs=[SM, ANY, ANY, VM, VM, VM, ANY],
        out_specs=[VM] * 3,
        scratch_shapes=[pltpu.SemaphoreType.DMA((2, 1))],
        compiler_params=params(8),
        cost_estimate=cost(2 * 256 * COLS * (TOK + COLS), 2 * MB),
        name="left_own",
    )(me, acts, error, qt, t3, came, after)
    return p0, {0: (acts_v, 0)}, {0: (err_v, 0)}


def memory_blocks(rs, held_a, held_e, grad_v, after, load=(), me=None, acts=None):
    n, m = len(rs), len(load)

    def body(*refs):
        g_ref, rest = refs[2 * n], refs[2 * n + 2 :]
        copies = []
        if m:
            me_ref, acts_hbm, sem = rest[0], rest[1], rest[-1]
            rest = rest[2:-1]
            copies = copies_in(me_ref, load, acts_hbm, rest[n], sem)
        for c in copies:
            c.start()
        for i, r in enumerate(rs):
            a_ref, e_ref = refs[2 * i : 2 * i + 2]
            grad = lax.dot_general(
                a_ref[held_a[r][1]], g_ref[...], TN, preferred_element_type=F32
            )
            rest[i][...] = grad + e_ref[held_e[r][1]].astype(F32)
        for c in copies:
            c.wait()

    shapes = [pltpu.VMEM((COLS, COLS), F32)] * n
    args = [x for r in rs for x in (held_a[r][0], held_e[r][0])] + [grad_v, after]
    in_specs = [VM] * (2 * n + 1) + [ANY]
    if m:
        shapes.append(pltpu.VMEM((m, TOK, COLS), BF16))
        args += [me, acts]
        in_specs += [SM, ANY]
    out = pl.pallas_call(
        body,
        out_shape=shapes,
        in_specs=in_specs,
        out_specs=[VM] * len(shapes),
        scratch_shapes=[pltpu.SemaphoreType.DMA((m,))] if m else [],
        compiler_params=params(8),
        cost_estimate=cost(2 * n * COLS * COLS * TOK),
        name="memory_blocks",
    )(*args)
    return dict(zip(rs, out)), {r: (out[n], k) for k, r in enumerate(load)}


def right(work, held_a, held_e, grad_v, earlier=None, last=False):
    n = len(work)

    def body(*refs):
        g_ref, rest = refs[3 * n], refs[3 * n + 1 :]
        given, outs = (rest[:3], rest[3:]) if earlier else ((), rest)
        tmp, q, gram = (x[...] for x in given) if earlier else (0.0, 0.0, 0.0)
        for i, (r, _, entry) in enumerate(work):
            block, a_ref, e_ref = refs[3 * i : 3 * i + 3]
            a, e = a_ref[held_a[r][1]], e_ref[held_e[r][1]]
            p = split3(block[...] if entry is None else block[entry])
            tmp = tmp + fold3(lax.dot_general(p, a, NT, preferred_element_type=F32))
            q = q + fold3(jnp.dot(p, e, preferred_element_type=F32))
            gram = gram + lax.dot_general(p, p, NT, preferred_element_type=F32)
        if last:
            q = q + fold3(jnp.dot(split3(tmp), g_ref[...], preferred_element_type=F32))
            outs[0][...] = q
            outs[1][...] = gram
        else:
            outs[0][...] = tmp
            outs[1][...] = q
            outs[2][...] = gram

    shapes = [
        jax.ShapeDtypeStruct((RANK, TOK), F32),
        jax.ShapeDtypeStruct((RANK, COLS), F32),
        jax.ShapeDtypeStruct((TRI, TRI), F32),
    ]
    if last:
        shapes = shapes[1:]
    args = [x for r, array, _ in work for x in (array, held_a[r][0], held_e[r][0])]
    args += [grad_v, *(earlier or ())]
    return pl.pallas_call(
        body,
        out_shape=shapes,
        in_specs=[VM] * len(args),
        out_specs=[VM] * len(shapes),
        compiler_params=params(8),
        cost_estimate=cost(2 * n * 256 * COLS * (TOK + COLS)),
        name="right_last" if last else "right_part",
    )(*args)


def orthonormal_body(gram_ref, *refs):
    blocks, theirs, p3_ref, inv_ref = refs[: HALF + 1], *refs[HALF + 1 :]
    wide = fold3(gram_ref[...])
    gram = wide[:, :RANK] + wide[:, RANK : 2 * RANK] + wide[:, 2 * RANK :]
    rows = lax.broadcasted_iota(jnp.int32, (RANK, RANK), 0)
    cols = lax.broadcasted_iota(jnp.int32, (RANK, RANK), 1)
    eye = (rows == cols).astype(F32)
    work = jnp.concatenate([gram, eye], axis=1)
    wide = (RANK, 2 * RANK)
    below = lax.broadcasted_iota(jnp.int32, wide, 0)
    for k in range(0, RANK, 8):
        col = [jnp.broadcast_to(work[:, k + i : k + i + 1], wide) for i in range(8)]
        row = [work[k + i : k + i + 1, :] for i in range(8)]
        factor = []
        for i in range(8):
            f = jnp.where(below > k + i, col[i] / col[i][k + i : k + i + 1, :], 0.0)
            factor.append(f)
            for j in range(i + 1, 8):
                col[j] = col[j] - f * col[j][k + i : k + i + 1, :]
                row[j] = row[j] - f[k + j : k + j + 1, :] * row[i]
        for f, r in zip(factor, row):
            work = work - f * r
    diag = jnp.sum(work[:, :RANK] * eye, axis=1, keepdims=True)
    inv = work[:, RANK:] / jnp.sqrt(diag)
    inv_ref[...] = inv
    for k in range(NBLK):
        block = theirs[k - HALF - 1] if k > HALF else blocks[k][...]
        p = jnp.dot(inv, block, precision=HIGH, preferred_element_type=F32)
        hi = p.astype(BF16).astype(F32)
        r = p - hi
        mid = r.astype(BF16).astype(F32)
        stacked = jnp.concatenate([hi, mid, r - mid, jnp.zeros_like(p)], axis=0)
        p3_ref[k] = stacked.T.astype(BF16)


def orthonormal(gram, blocks, theirs):
    return pl.pallas_call(
        orthonormal_body,
        out_shape=(
            pltpu.VMEM((NBLK, COLS, 4 * RANK), BF16),
            jax.ShapeDtypeStruct((RANK, RANK), F32),
        ),
        in_specs=[VM] * (3 + HALF),
        out_specs=(VM, VM),
        compiler_params=params(8),
        cost_estimate=cost(1 << 31),
        name="orthonormal",
    )(gram, *blocks, theirs)


def update_body(me_ref, a_ref, b_ref, c_ref, d_ref, inv_ref, dither_ref, p3_ref, *rest):
    mem = rest[:NBLK]
    qf_ref, out_hbm, stage, sem = rest[NBLK:]
    total = (a_ref[...] + b_ref[...]) + (c_ref[...] + d_ref[...])
    qmat = jnp.dot(inv_ref[...], total, precision=HIGH, preferred_element_type=F32) / WORKERS
    scale = 1.0 + (dither_ref[...].astype(F32) / 65536.0 - 0.5) / 4.0
    qt = (qmat * scale).astype(BF16)
    qf_ref[...] = qt
    q3 = jnp.concatenate([qt, qt, qt, jnp.zeros((RANK, COLS), BF16)], axis=0)
    copies = []
    for k, r in enumerate(ORDER):
        approx = jnp.dot(p3_ref[k], q3, preferred_element_type=F32)
        stage[k] = (mem[k][...] - approx).astype(BF16)
        at = pl.ds(rows_of(me_ref[0], r), COLS)
        copies.append(pltpu.make_async_copy(stage.at[k], out_hbm.at[at, :], sem.at[k]))
        copies[-1].start()
    for c in copies:
        c.wait()


def update(me, parts, inv, dither, p3, memory):
    return pl.pallas_call(
        update_body,
        out_shape=(
            jax.ShapeDtypeStruct((RANK, COLS), BF16),
            jax.ShapeDtypeStruct((D, COLS), BF16),
        ),
        in_specs=[SM] + [VM] * (len(parts) + 3 + NBLK),
        out_specs=(VM, ANY),
        scratch_shapes=[
            pltpu.VMEM((NBLK, COLS, COLS), BF16),
            pltpu.SemaphoreType.DMA((NBLK,)),
        ],
        compiler_params=params(16),
        cost_estimate=cost(2 * D * COLS * 256, 7 * MB),
        name="update",
    )(me, *parts, inv, dither, p3, *memory)


def sum_after(parts, after):
    n = len(parts)

    def body(*refs):
        total = refs[0][...]
        for x in refs[1:n]:
            total = total + x[...]
        refs[-1][...] = total

    return pl.pallas_call(
        body,
        out_shape=jax.ShapeDtypeStruct((RANK, COLS), F32),
        in_specs=[VM] * n + [ANY] * len(after),
        out_specs=VM,
        compiler_params=params(8),
        cost_estimate=cost(1000),
        name="sum_after",
    )(*parts, *after)


def stack_after(parts, after):
    n = len(parts)

    def body(*refs):
        for i in range(n):
            refs[-1][i] = refs[i][...]

    return pl.pallas_call(
        body,
        out_shape=jax.ShapeDtypeStruct((n, RANK, COLS), F32),
        in_specs=[VM] * n + [ANY] * len(after),
        out_specs=VM,
        compiler_params=params(8),
        cost_estimate=cost(1000),
        name="stack_after",
    )(*parts, *after)


def place(y, x, z, core):
    return ((y * 4 + x) * 4 + z) * 2 + core


def exchange(v, axes, r):
    pairs = []
    for source in range(128):
        at = {"y": source >> 5, "x": source >> 3 & 3, "z": source >> 1 & 3}
        at[axes[source & 1]] ^= r
        pairs.append((source, place(core=source & 1, **at)))
    return lax.ppermute(v, ("dp", "tensor"), pairs)


def ring(v, axes):
    return [exchange(v, axes, r) for r in RING]


def core(v):
    return lax.ppermute(v, ("dp", "tensor"), [(i, i ^ 1) for i in range(128)])


def per_device(acts, out_grad, error, q_seed, dither):
    me = lax.axis_index(("dp", "tensor")).astype(jnp.int32).reshape(1)
    acts = pltpu.with_memory_space_constraint(acts, pltpu.HBM)
    error = pltpu.with_memory_space_constraint(error, pltpu.HBM)
    out_grad = pltpu.with_memory_space_constraint(out_grad, pltpu.HBM)
    seed = pltpu.with_memory_space_constraint(q_seed.T, pltpu.HBM)

    away, held_e, grad_v, qt = left_away(me, error, out_grad, seed)
    came = core(away)
    kept, held_a, more_e = left_kept(me, acts, error, qt)
    held_e |= more_e
    part, t3 = left_sum(held_a[2][0], kept, away, came)
    from_ring = [exchange(part[r - 1], OWNER, r) for r in RING]
    own, more_a, more_e = left_own(me, acts, error, qt, t3, came, part)
    held_a |= more_a
    held_e |= more_e
    memory = {}

    def memory_of(rs, after, load=()):
        blocks, more = memory_blocks(rs, held_a, held_e, grad_v, after, load, me, acts)
        memory.update(blocks)
        held_a.update(more)

    memory_of((2,), part)
    own = sum_after([own, *from_ring], [memory[2]])

    from_ring = ring(own, SECOND)
    memory_of((0,), own, (1, 3, 5))
    own = sum_after([own, *from_ring], [memory[0]])
    from_ring = ring(own, THIRD)
    memory_of((4, 1), own, (7,))
    own = sum_after([own, *from_ring], [memory[4]])

    other = core(own)
    mine = ring(own, OWNER)
    held = (held_a, held_e, grad_v)
    early = right([(0, own, None), (1, other, None)], *held)
    early = right([(2 * RING[2], mine[2], None)], *held, early)
    theirs = core(stack_after(mine, [early[0]]))
    mid = right([(2 * r, x, None) for r, x in zip(RING[:2], mine)], *held, early)
    q, gram = right([(2 * r + 1, theirs, i) for i, r in enumerate(RING)], *held, mid, True)

    from_ring = ring(q, DP_FIRST)
    p3, inv = orthonormal(gram, [own, other, *mine], theirs)
    memory_of((3,), q)
    q = sum_after([q, *from_ring], [inv, memory[3]])
    from_ring = ring(q, DP_SECOND)
    memory_of((5, 6, 7), q)
    q_factor, new_error = update(me, [q, *from_ring], inv, dither.T, p3, [memory[r] for r in ORDER])
    return (q_factor.T, new_error)


def solution(mesh):
    in_specs = (
        P("dp", None),
        P("dp", "tensor"),
        P("dp", "tensor"),
        P("tensor", None),
        P("tensor", None),
    )
    out_specs = (P("tensor", None), P("dp", "tensor"))
    return jax.shard_map(
        per_device, mesh=mesh, in_specs=in_specs, out_specs=out_specs, check_vma=False
    )
```

```python
import jax
import jax.numpy as jnp
from jax import lax
from jax.experimental import pallas as pl
from jax.experimental.pallas import tpu as pltpu
from jax.sharding import PartitionSpec as P

HIGH = lax.Precision.HIGHEST
F32 = jnp.float32
BF16 = jnp.bfloat16

D = 5120
TOK = 1024
COLS = 640
RANK = 32
TRI = 3 * RANK
NBLK = 8
HALF = 4
WORKERS = 16
MB = 1 << 20
RING = (1, 2, 3)
OWNER, SECOND, THIRD = "xz", "yx", "zy"
DP_FIRST, DP_SECOND = "xy", "yx"
ORDER = (0, 1, *(2 * r for r in RING), *(2 * r + 1 for r in RING))

NT = (((1,), (1,)), ((), ()))
TN = (((0,), (0,)), ((), ()))

VM = pl.BlockSpec(memory_space=pltpu.VMEM)
SM = pl.BlockSpec(memory_space=pltpu.SMEM)
ANY = pl.BlockSpec(memory_space=pl.ANY)


def params(mb):
    return pltpu.CompilerParams(vmem_limit_bytes=mb * MB)


def cost(flops, bytes_accessed=0):
    return pl.CostEstimate(flops=flops, bytes_accessed=bytes_accessed, transcendentals=0)


def split3(x):
    hi = x.astype(BF16)
    r = x - hi.astype(F32)
    mid = r.astype(BF16)
    lo = (r - mid.astype(F32)).astype(BF16)
    return jnp.concatenate([hi, mid, lo], axis=0)


def fold3(y):
    return y[:RANK] + y[RANK : 2 * RANK] + y[2 * RANK :]


def rows_of(me, r):
    core = (me ^ r) & 1
    z, x = (me >> 1) & 3, (me >> 3) & 3
    block = ((x + core * (z - x)) ^ (r >> 1)) * 2 + core
    return pl.multiple_of(block * COLS, COLS)


def copies_in(me_ref, rs, acts_hbm, acts_v, sem):
    return [
        pltpu.make_async_copy(
            acts_hbm.at[:, pl.ds(rows_of(me_ref[0], r), COLS)], acts_v.at[k], sem.at[k]
        )
        for k, r in enumerate(rs)
    ]


def copies_in_rows(me_ref, rs, err_hbm, err_v, sem):
    return [
        pltpu.make_async_copy(
            err_hbm.at[pl.ds(rows_of(me_ref[0], r), COLS), :], err_v.at[k], sem.at[k]
        )
        for k, r in enumerate(rs)
    ]


def left_away(me, error, out_grad, seed):
    rs = (1, 3, 5, 7)

    def body(me_ref, err_hbm, grad_hbm, seed_hbm, away, err_v, grad_v, qt_ref, sem, more, seed_v):
        seed_copy = pltpu.make_async_copy(seed_hbm, seed_v, more.at[0])
        grad_copy = pltpu.make_async_copy(grad_hbm, grad_v, more.at[1])
        err_copy = copies_in_rows(me_ref, rs, err_hbm, err_v, sem)
        seed_copy.start()
        err_copy[0].start()
        err_copy[1].start()
        grad_copy.start()
        seed_copy.wait()
        qt = seed_v[...].astype(F32).astype(BF16)
        qt_ref[...] = qt

        def multiply(k):
            err_copy[k].wait()
            if k + 2 < HALF:
                err_copy[k + 2].start()
            away[:, k * COLS : (k + 1) * COLS] = lax.dot_general(
                qt, err_v[k], NT, preferred_element_type=F32
            )

        multiply(0)
        multiply(1)
        grad_copy.wait()
        away[:, HALF * COLS :] = lax.dot_general(
            qt, grad_v[...], NT, preferred_element_type=F32
        )
        multiply(2)
        multiply(3)

    away, err_v, grad_v, qt = pl.pallas_call(
        body,
        out_shape=[
            jax.ShapeDtypeStruct((RANK, HALF * COLS + TOK), F32),
            pltpu.VMEM((HALF, COLS, COLS), BF16),
            pltpu.VMEM((TOK, COLS), BF16),
            pltpu.VMEM((RANK, COLS), BF16),
        ],
        in_specs=[SM, ANY, ANY, ANY],
        out_specs=[VM] * 4,
        scratch_shapes=[
            pltpu.SemaphoreType.DMA((HALF,)),
            pltpu.SemaphoreType.DMA((2,)),
            pltpu.VMEM((RANK, COLS), jnp.int32),
        ],
        compiler_params=params(8),
        cost_estimate=cost(2 * HALF * 256 * COLS * COLS, 5 * MB),
        name="left_away",
    )(me, error, out_grad, seed)
    return away, {r: (err_v, k) for k, r in enumerate(rs)}, grad_v, qt


def left_kept(me, acts, error, qt):
    rs = (2, 4, 6)

    def body(me_ref, acts_hbm, err_hbm, qt_ref, kept, acts_v, err_v, sem, acts_sem):
        err_copy = copies_in_rows(me_ref, rs, err_hbm, err_v, sem)
        acts_copy = copies_in(me_ref, rs, acts_hbm, acts_v, acts_sem)
        for c in err_copy + acts_copy:
            c.start()
        for k, c in enumerate(err_copy):
            c.wait()
            kept[k] = lax.dot_general(qt_ref[...], err_v[k], NT, preferred_element_type=F32)
        for c in acts_copy:
            c.wait()

    kept, acts_v, err_v = pl.pallas_call(
        body,
        out_shape=[
            jax.ShapeDtypeStruct((3, RANK, COLS), F32),
            pltpu.VMEM((3, TOK, COLS), BF16),
            pltpu.VMEM((3, COLS, COLS), BF16),
        ],
        in_specs=[SM, ANY, ANY, VM],
        out_specs=[VM] * 3,
        scratch_shapes=[pltpu.SemaphoreType.DMA((3,)), pltpu.SemaphoreType.DMA((3,))],
        compiler_params=params(8),
        cost_estimate=cost(2 * 3 * 256 * COLS * COLS, 6 * MB),
        name="left_kept",
    )(me, acts, error, qt)
    return kept, {r: (acts_v, k) for k, r in enumerate(rs)}, {r: (err_v, k) for k, r in enumerate(rs)}


def left_sum(acts_v, kept, away, came):
    def body(acts_v, kept, away, came, part, t3_ref):
        t3_ref[...] = split3(away[:, HALF * COLS :] + came[:, HALF * COLS :])
        for k in range(3):
            p = fold3(jnp.dot(t3_ref[...], acts_v[k], preferred_element_type=F32))
            p = p + (kept[k] + came[:, (k + 1) * COLS : (k + 2) * COLS])
            part[k] = p * (1.0 / 32.0)

    return pl.pallas_call(
        body,
        out_shape=[
            jax.ShapeDtypeStruct((3, RANK, COLS), F32),
            pltpu.VMEM((TRI, TOK), BF16),
        ],
        in_specs=[VM] * 4,
        out_specs=[VM] * 2,
        compiler_params=params(8),
        cost_estimate=cost(2 * 3 * 256 * COLS * TOK),
        name="left_sum",
    )(acts_v, kept, away, came)


def left_own(me, acts, error, qt, t3, came, after):
    def body(me_ref, acts_hbm, err_hbm, qt_ref, t3_ref, came, after_ref, p0, acts_v, err_v, sem):
        err_copy = copies_in_rows(me_ref, (0,), err_hbm, err_v, sem.at[0])
        acts_copy = copies_in(me_ref, (0,), acts_hbm, acts_v, sem.at[1])
        err_copy[0].start()
        acts_copy[0].start()
        err_copy[0].wait()
        p = lax.dot_general(qt_ref[...], err_v[0], NT, preferred_element_type=F32)
        p = p + came[:, :COLS]
        acts_copy[0].wait()
        p = p + fold3(jnp.dot(t3_ref[...], acts_v[0], preferred_element_type=F32))
        p0[...] = p * (1.0 / 32.0)

    p0, acts_v, err_v = pl.pallas_call(
        body,
        out_shape=[
            jax.ShapeDtypeStruct((RANK, COLS), F32),
            pltpu.VMEM((1, TOK, COLS), BF16),
            pltpu.VMEM((1, COLS, COLS), BF16),
        ],
        in_specs=[SM, ANY, ANY, VM, VM, VM, ANY],
        out_specs=[VM] * 3,
        scratch_shapes=[pltpu.SemaphoreType.DMA((2, 1))],
        compiler_params=params(8),
        cost_estimate=cost(2 * 256 * COLS * (TOK + COLS), 2 * MB),
        name="left_own",
    )(me, acts, error, qt, t3, came, after)
    return p0, {0: (acts_v, 0)}, {0: (err_v, 0)}


def memory_blocks(rs, held_a, held_e, grad_v, after, load=(), me=None, acts=None):
    n, m = len(rs), len(load)

    def body(*refs):
        g_ref, rest = refs[2 * n], refs[2 * n + 2 :]
        copies = []
        if m:
            me_ref, acts_hbm, sem = rest[0], rest[1], rest[-1]
            rest = rest[2:-1]
            copies = copies_in(me_ref, load, acts_hbm, rest[n], sem)
        for c in copies:
            c.start()
        for i, r in enumerate(rs):
            a_ref, e_ref = refs[2 * i : 2 * i + 2]
            grad = lax.dot_general(
                a_ref[held_a[r][1]], g_ref[...], TN, preferred_element_type=F32
            )
            rest[i][...] = grad + e_ref[held_e[r][1]].astype(F32)
        for c in copies:
            c.wait()

    shapes = [pltpu.VMEM((COLS, COLS), F32)] * n
    args = [x for r in rs for x in (held_a[r][0], held_e[r][0])] + [grad_v, after]
    in_specs = [VM] * (2 * n + 1) + [ANY]
    if m:
        shapes.append(pltpu.VMEM((m, TOK, COLS), BF16))
        args += [me, acts]
        in_specs += [SM, ANY]
    out = pl.pallas_call(
        body,
        out_shape=shapes,
        in_specs=in_specs,
        out_specs=[VM] * len(shapes),
        scratch_shapes=[pltpu.SemaphoreType.DMA((m,))] if m else [],
        compiler_params=params(8),
        cost_estimate=cost(2 * n * COLS * COLS * TOK),
        name="memory_blocks",
    )(*args)
    return dict(zip(rs, out)), {r: (out[n], k) for k, r in enumerate(load)}


def right(work, held_a, held_e, grad_v, earlier=None, last=False):
    n = len(work)

    def body(*refs):
        g_ref, rest = refs[3 * n], refs[3 * n + 1 :]
        given, outs = (rest[:3], rest[3:]) if earlier else ((), rest)
        tmp, q, gram = (x[...] for x in given) if earlier else (0.0, 0.0, 0.0)
        for i, (r, _, entry) in enumerate(work):
            block, a_ref, e_ref = refs[3 * i : 3 * i + 3]
            a, e = a_ref[held_a[r][1]], e_ref[held_e[r][1]]
            p = split3(block[...] if entry is None else block[entry])
            tmp = tmp + fold3(lax.dot_general(p, a, NT, preferred_element_type=F32))
            q = q + fold3(jnp.dot(p, e, preferred_element_type=F32))
            gram = gram + lax.dot_general(p, p, NT, preferred_element_type=F32)
        if last:
            q = q + fold3(jnp.dot(split3(tmp), g_ref[...], preferred_element_type=F32))
            outs[0][...] = q
            outs[1][...] = gram
        else:
            outs[0][...] = tmp
            outs[1][...] = q
            outs[2][...] = gram

    shapes = [
        jax.ShapeDtypeStruct((RANK, TOK), F32),
        jax.ShapeDtypeStruct((RANK, COLS), F32),
        jax.ShapeDtypeStruct((TRI, TRI), F32),
    ]
    if last:
        shapes = shapes[1:]
    args = [x for r, array, _ in work for x in (array, held_a[r][0], held_e[r][0])]
    args += [grad_v, *(earlier or ())]
    return pl.pallas_call(
        body,
        out_shape=shapes,
        in_specs=[VM] * len(args),
        out_specs=[VM] * len(shapes),
        compiler_params=params(8),
        cost_estimate=cost(2 * n * 256 * COLS * (TOK + COLS)),
        name="right_last" if last else "right_part",
    )(*args)


def orthonormal_body(gram_ref, *refs):
    blocks, theirs, p3_ref, inv_ref = refs[: HALF + 1], *refs[HALF + 1 :]
    wide = fold3(gram_ref[...])
    gram = wide[:, :RANK] + wide[:, RANK : 2 * RANK] + wide[:, 2 * RANK :]
    rows = lax.broadcasted_iota(jnp.int32, (RANK, RANK), 0)
    cols = lax.broadcasted_iota(jnp.int32, (RANK, RANK), 1)
    eye = (rows == cols).astype(F32)
    work = jnp.concatenate([gram, eye], axis=1)
    wide = (RANK, 2 * RANK)
    below = lax.broadcasted_iota(jnp.int32, wide, 0)
    for k in range(0, RANK, 8):
        col = [jnp.broadcast_to(work[:, k + i : k + i + 1], wide) for i in range(8)]
        row = [work[k + i : k + i + 1, :] for i in range(8)]
        factor = []
        for i in range(8):
            f = jnp.where(below > k + i, col[i] / col[i][k + i : k + i + 1, :], 0.0)
            factor.append(f)
            for j in range(i + 1, 8):
                col[j] = col[j] - f * col[j][k + i : k + i + 1, :]
                row[j] = row[j] - f[k + j : k + j + 1, :] * row[i]
        for f, r in zip(factor, row):
            work = work - f * r
    diag = jnp.sum(work[:, :RANK] * eye, axis=1, keepdims=True)
    inv = work[:, RANK:] / jnp.sqrt(diag)
    inv_ref[...] = inv
    for k in range(NBLK):
        block = theirs[k - HALF - 1] if k > HALF else blocks[k][...]
        p = jnp.dot(inv, block, precision=HIGH, preferred_element_type=F32)
        hi = p.astype(BF16).astype(F32)
        r = p - hi
        mid = r.astype(BF16).astype(F32)
        stacked = jnp.concatenate([hi, mid, r - mid, jnp.zeros_like(p)], axis=0)
        p3_ref[k] = stacked.T.astype(BF16)


def orthonormal(gram, blocks, theirs):
    return pl.pallas_call(
        orthonormal_body,
        out_shape=(
            pltpu.VMEM((NBLK, COLS, 4 * RANK), BF16),
            jax.ShapeDtypeStruct((RANK, RANK), F32),
        ),
        in_specs=[VM] * (3 + HALF),
        out_specs=(VM, VM),
        compiler_params=params(8),
        cost_estimate=cost(1 << 31),
        name="orthonormal",
    )(gram, *blocks, theirs)


def update_body(me_ref, a_ref, b_ref, c_ref, d_ref, inv_ref, dither_ref, p3_ref, *rest):
    mem = rest[:NBLK]
    qf_ref, out_hbm, stage, sem = rest[NBLK:]
    total = (a_ref[...] + b_ref[...]) + (c_ref[...] + d_ref[...])
    qmat = jnp.dot(inv_ref[...], total, precision=HIGH, preferred_element_type=F32) / WORKERS
    scale = 1.0 + (dither_ref[...].astype(F32) / 65536.0 - 0.5) / 4.0
    qt = (qmat * scale).astype(BF16)
    qf_ref[...] = qt
    q3 = jnp.concatenate([qt, qt, qt, jnp.zeros((RANK, COLS), BF16)], axis=0)
    copies = []
    half = COLS // 2
    for k, r in enumerate(ORDER):
        for i in range(2):
            rows = pl.ds(i * half, half)
            approx = jnp.dot(p3_ref[k, rows], q3, preferred_element_type=F32)
            stage[k, rows] = (mem[k][rows] - approx).astype(BF16)
            at = pl.ds(pl.multiple_of(rows_of(me_ref[0], r) + i * half, half), half)
            copies.append(
                pltpu.make_async_copy(stage.at[k, rows], out_hbm.at[at, :], sem.at[2 * k + i])
            )
            copies[-1].start()
    for c in copies:
        c.wait()


def update(me, parts, inv, dither, p3, memory):
    return pl.pallas_call(
        update_body,
        out_shape=(
            jax.ShapeDtypeStruct((RANK, COLS), BF16),
            jax.ShapeDtypeStruct((D, COLS), BF16),
        ),
        in_specs=[SM] + [VM] * (len(parts) + 3 + NBLK),
        out_specs=(VM, ANY),
        scratch_shapes=[
            pltpu.VMEM((NBLK, COLS, COLS), BF16),
            pltpu.SemaphoreType.DMA((2 * NBLK,)),
        ],
        compiler_params=params(16),
        cost_estimate=cost(2 * D * COLS * 256, 7 * MB),
        name="update",
    )(me, *parts, inv, dither, p3, *memory)


def sum_after(parts, after):
    n = len(parts)

    def body(*refs):
        total = refs[0][...]
        for x in refs[1:n]:
            total = total + x[...]
        refs[-1][...] = total

    return pl.pallas_call(
        body,
        out_shape=jax.ShapeDtypeStruct((RANK, COLS), F32),
        in_specs=[VM] * n + [ANY] * len(after),
        out_specs=VM,
        compiler_params=params(8),
        cost_estimate=cost(1000),
        name="sum_after",
    )(*parts, *after)


def stack_after(parts, after):
    n = len(parts)

    def body(*refs):
        for i in range(n):
            refs[-1][i] = refs[i][...]

    return pl.pallas_call(
        body,
        out_shape=jax.ShapeDtypeStruct((n, RANK, COLS), F32),
        in_specs=[VM] * n + [ANY] * len(after),
        out_specs=VM,
        compiler_params=params(8),
        cost_estimate=cost(1000),
        name="stack_after",
    )(*parts, *after)


def place(y, x, z, core):
    return ((y * 4 + x) * 4 + z) * 2 + core


def exchange(v, axes, r):
    pairs = []
    for source in range(128):
        at = {"y": source >> 5, "x": source >> 3 & 3, "z": source >> 1 & 3}
        at[axes[source & 1]] ^= r
        pairs.append((source, place(core=source & 1, **at)))
    return lax.ppermute(v, ("dp", "tensor"), pairs)


def ring(v, axes):
    return [exchange(v, axes, r) for r in RING]


def core(v):
    return lax.ppermute(v, ("dp", "tensor"), [(i, i ^ 1) for i in range(128)])


def per_device(acts, out_grad, error, q_seed, dither):
    me = lax.axis_index(("dp", "tensor")).astype(jnp.int32).reshape(1)
    acts = pltpu.with_memory_space_constraint(acts, pltpu.HBM)
    error = pltpu.with_memory_space_constraint(error, pltpu.HBM)
    out_grad = pltpu.with_memory_space_constraint(out_grad, pltpu.HBM)
    seed = pltpu.with_memory_space_constraint(q_seed.T, pltpu.HBM)

    away, held_e, grad_v, qt = left_away(me, error, out_grad, seed)
    came = core(away)
    kept, held_a, more_e = left_kept(me, acts, error, qt)
    held_e |= more_e
    part, t3 = left_sum(held_a[2][0], kept, away, came)
    from_ring = [exchange(part[r - 1], OWNER, r) for r in RING]
    own, more_a, more_e = left_own(me, acts, error, qt, t3, came, part)
    held_a |= more_a
    held_e |= more_e
    memory = {}

    def memory_of(rs, after, load=()):
        blocks, more = memory_blocks(rs, held_a, held_e, grad_v, after, load, me, acts)
        memory.update(blocks)
        held_a.update(more)

    memory_of((2,), part)
    own = sum_after([own, *from_ring], [memory[2]])

    from_ring = ring(own, SECOND)
    memory_of((0,), own, (1, 3, 5))
    own = sum_after([own, *from_ring], [memory[0]])
    from_ring = ring(own, THIRD)
    memory_of((4, 1), own, (7,))
    own = sum_after([own, *from_ring], [memory[4]])

    other = core(own)
    mine = ring(own, OWNER)
    memory_of((6,), own)
    held = (held_a, held_e, grad_v)
    early = right([(0, own, None), (1, other, None)], *held)
    early = right([(2 * RING[2], mine[2], None)], *held, early)
    theirs = core(stack_after(mine, [early[0], memory[6]]))
    mid = right([(2 * r, x, None) for r, x in zip(RING[:2], mine)], *held, early)
    q, gram = right([(2 * r + 1, theirs, i) for i, r in enumerate(RING)], *held, mid, True)

    from_ring = ring(q, DP_FIRST)
    p3, inv = orthonormal(gram, [own, other, *mine], theirs)
    memory_of((3,), q)
    q = sum_after([q, *from_ring], [inv, memory[3]])
    from_ring = ring(q, DP_SECOND)
    memory_of((5, 7), q)
    q_factor, new_error = update(me, [q, *from_ring], inv, dither.T, p3, [memory[r] for r in ORDER])
    return (q_factor.T, new_error)


def solution(mesh):
    in_specs = (
        P("dp", None),
        P("dp", "tensor"),
        P("dp", "tensor"),
        P("tensor", None),
        P("tensor", None),
    )
    out_specs = (P("tensor", None), P("dp", "tensor"))
    return jax.shard_map(
        per_device, mesh=mesh, in_specs=in_specs, out_specs=out_specs, check_vma=False
    )
```

```python
import jax
import jax.numpy as jnp
from jax import lax
from jax.experimental import pallas as pl
from jax.experimental.pallas import tpu as pltpu
from jax.sharding import PartitionSpec as P

HIGH = lax.Precision.HIGHEST
F32 = jnp.float32
BF16 = jnp.bfloat16

D = 5120
TOK = 1024
COLS = 640
RANK = 32
TRI = 3 * RANK
NBLK = 8
HALF = 4
WORKERS = 16
MB = 1 << 20
RING = (1, 2, 3)
OWNER, SECOND, THIRD = "xz", "yx", "zy"
DP_FIRST, DP_SECOND = "xy", "yx"
ORDER = (0, 1, *(2 * r for r in RING), *(2 * r + 1 for r in RING))

NT = (((1,), (1,)), ((), ()))
TN = (((0,), (0,)), ((), ()))

VM = pl.BlockSpec(memory_space=pltpu.VMEM)
SM = pl.BlockSpec(memory_space=pltpu.SMEM)
ANY = pl.BlockSpec(memory_space=pl.ANY)


def params(mb):
    return pltpu.CompilerParams(vmem_limit_bytes=mb * MB)


def cost(flops, bytes_accessed=0):
    return pl.CostEstimate(flops=flops, bytes_accessed=bytes_accessed, transcendentals=0)


def split3(x):
    hi = x.astype(BF16)
    r = x - hi.astype(F32)
    mid = r.astype(BF16)
    lo = (r - mid.astype(F32)).astype(BF16)
    return jnp.concatenate([hi, mid, lo], axis=0)


def fold3(y):
    return y[:RANK] + y[RANK : 2 * RANK] + y[2 * RANK :]


def rows_of(me, r):
    core = (me ^ r) & 1
    z, x = (me >> 1) & 3, (me >> 3) & 3
    block = ((x + core * (z - x)) ^ (r >> 1)) * 2 + core
    return pl.multiple_of(block * COLS, COLS)


def copies_in(me_ref, rs, acts_hbm, acts_v, sem):
    return [
        pltpu.make_async_copy(
            acts_hbm.at[:, pl.ds(rows_of(me_ref[0], r), COLS)], acts_v.at[k], sem.at[k]
        )
        for k, r in enumerate(rs)
    ]


def copies_in_rows(me_ref, rs, err_hbm, err_v, sem):
    return [
        pltpu.make_async_copy(
            err_hbm.at[pl.ds(rows_of(me_ref[0], r), COLS), :], err_v.at[k], sem.at[k]
        )
        for k, r in enumerate(rs)
    ]


def left_away(me, error, out_grad, seed):
    rs = (1, 3, 5, 7)

    def body(me_ref, err_hbm, grad_hbm, seed_hbm, away, err_v, grad_v, qt_ref, sem, more, seed_v):
        seed_copy = pltpu.make_async_copy(seed_hbm, seed_v, more.at[0])
        grad_copy = pltpu.make_async_copy(grad_hbm, grad_v, more.at[1])
        err_copy = copies_in_rows(me_ref, rs, err_hbm, err_v, sem)
        seed_copy.start()
        err_copy[0].start()
        err_copy[1].start()
        grad_copy.start()
        seed_copy.wait()
        qt = seed_v[...].astype(F32).astype(BF16)
        qt_ref[...] = qt

        def multiply(k):
            err_copy[k].wait()
            if k + 2 < HALF:
                err_copy[k + 2].start()
            away[:, k * COLS : (k + 1) * COLS] = lax.dot_general(
                qt, err_v[k], NT, preferred_element_type=F32
            )

        multiply(0)
        multiply(1)
        grad_copy.wait()
        away[:, HALF * COLS :] = lax.dot_general(
            qt, grad_v[...], NT, preferred_element_type=F32
        )
        multiply(2)
        multiply(3)

    away, err_v, grad_v, qt = pl.pallas_call(
        body,
        out_shape=[
            jax.ShapeDtypeStruct((RANK, HALF * COLS + TOK), F32),
            pltpu.VMEM((HALF, COLS, COLS), BF16),
            pltpu.VMEM((TOK, COLS), BF16),
            pltpu.VMEM((RANK, COLS), BF16),
        ],
        in_specs=[SM, ANY, ANY, ANY],
        out_specs=[VM] * 4,
        scratch_shapes=[
            pltpu.SemaphoreType.DMA((HALF,)),
            pltpu.SemaphoreType.DMA((2,)),
            pltpu.VMEM((RANK, COLS), jnp.int32),
        ],
        compiler_params=params(8),
        cost_estimate=cost(2 * HALF * 256 * COLS * COLS, 5 * MB),
        name="left_away",
    )(me, error, out_grad, seed)
    return away, {r: (err_v, k) for k, r in enumerate(rs)}, grad_v, qt


def left_kept(me, acts, error, qt):
    rs = (2, 4, 6)

    def body(me_ref, acts_hbm, err_hbm, qt_ref, kept, acts_v, err_v, sem, acts_sem):
        err_copy = copies_in_rows(me_ref, rs, err_hbm, err_v, sem)
        acts_copy = copies_in(me_ref, rs, acts_hbm, acts_v, acts_sem)
        for c in err_copy + acts_copy:
            c.start()
        for k, c in enumerate(err_copy):
            c.wait()
            kept[k] = lax.dot_general(qt_ref[...], err_v[k], NT, preferred_element_type=F32)
        for c in acts_copy:
            c.wait()

    kept, acts_v, err_v = pl.pallas_call(
        body,
        out_shape=[
            jax.ShapeDtypeStruct((3, RANK, COLS), F32),
            pltpu.VMEM((3, TOK, COLS), BF16),
            pltpu.VMEM((3, COLS, COLS), BF16),
        ],
        in_specs=[SM, ANY, ANY, VM],
        out_specs=[VM] * 3,
        scratch_shapes=[pltpu.SemaphoreType.DMA((3,)), pltpu.SemaphoreType.DMA((3,))],
        compiler_params=params(8),
        cost_estimate=cost(2 * 3 * 256 * COLS * COLS, 6 * MB),
        name="left_kept",
    )(me, acts, error, qt)
    return kept, {r: (acts_v, k) for k, r in enumerate(rs)}, {r: (err_v, k) for k, r in enumerate(rs)}


def left_sum(acts_v, kept, away, came):
    def body(acts_v, kept, away, came, part, t3_ref):
        t3_ref[...] = split3(away[:, HALF * COLS :] + came[:, HALF * COLS :])
        for k in range(3):
            p = fold3(jnp.dot(t3_ref[...], acts_v[k], preferred_element_type=F32))
            p = p + (kept[k] + came[:, (k + 1) * COLS : (k + 2) * COLS])
            part[k] = p * (1.0 / 32.0)

    return pl.pallas_call(
        body,
        out_shape=[
            jax.ShapeDtypeStruct((3, RANK, COLS), F32),
            pltpu.VMEM((TRI, TOK), BF16),
        ],
        in_specs=[VM] * 4,
        out_specs=[VM] * 2,
        compiler_params=params(8),
        cost_estimate=cost(2 * 3 * 256 * COLS * TOK),
        name="left_sum",
    )(acts_v, kept, away, came)


def left_own(me, acts, error, qt, t3, came, after):
    def body(me_ref, acts_hbm, err_hbm, qt_ref, t3_ref, came, after_ref, p0, acts_v, err_v, sem):
        err_copy = copies_in_rows(me_ref, (0,), err_hbm, err_v, sem.at[0])
        acts_copy = copies_in(me_ref, (0,), acts_hbm, acts_v, sem.at[1])
        err_copy[0].start()
        acts_copy[0].start()
        err_copy[0].wait()
        p = lax.dot_general(qt_ref[...], err_v[0], NT, preferred_element_type=F32)
        p = p + came[:, :COLS]
        acts_copy[0].wait()
        p = p + fold3(jnp.dot(t3_ref[...], acts_v[0], preferred_element_type=F32))
        p0[...] = p * (1.0 / 32.0)

    p0, acts_v, err_v = pl.pallas_call(
        body,
        out_shape=[
            jax.ShapeDtypeStruct((RANK, COLS), F32),
            pltpu.VMEM((1, TOK, COLS), BF16),
            pltpu.VMEM((1, COLS, COLS), BF16),
        ],
        in_specs=[SM, ANY, ANY, VM, VM, VM, ANY],
        out_specs=[VM] * 3,
        scratch_shapes=[pltpu.SemaphoreType.DMA((2, 1))],
        compiler_params=params(8),
        cost_estimate=cost(2 * 256 * COLS * (TOK + COLS), 2 * MB),
        name="left_own",
    )(me, acts, error, qt, t3, came, after)
    return p0, {0: (acts_v, 0)}, {0: (err_v, 0)}


def memory_blocks(rs, held_a, held_e, grad_v, after, load=(), me=None, acts=None):
    n, m = len(rs), len(load)

    def body(*refs):
        g_ref, rest = refs[2 * n], refs[2 * n + 2 :]
        copies = []
        if m:
            me_ref, acts_hbm, sem = rest[0], rest[1], rest[-1]
            rest = rest[2:-1]
            copies = copies_in(me_ref, load, acts_hbm, rest[n], sem)
        for c in copies:
            c.start()
        for i, r in enumerate(rs):
            a_ref, e_ref = refs[2 * i : 2 * i + 2]
            grad = lax.dot_general(
                a_ref[held_a[r][1]], g_ref[...], TN, preferred_element_type=F32
            )
            rest[i][...] = grad + e_ref[held_e[r][1]].astype(F32)
        for c in copies:
            c.wait()

    shapes = [pltpu.VMEM((COLS, COLS), F32)] * n
    args = [x for r in rs for x in (held_a[r][0], held_e[r][0])] + [grad_v, after]
    in_specs = [VM] * (2 * n + 1) + [ANY]
    if m:
        shapes.append(pltpu.VMEM((m, TOK, COLS), BF16))
        args += [me, acts]
        in_specs += [SM, ANY]
    out = pl.pallas_call(
        body,
        out_shape=shapes,
        in_specs=in_specs,
        out_specs=[VM] * len(shapes),
        scratch_shapes=[pltpu.SemaphoreType.DMA((m,))] if m else [],
        compiler_params=params(8),
        cost_estimate=cost(2 * n * COLS * COLS * TOK),
        name="memory_blocks",
    )(*args)
    return dict(zip(rs, out)), {r: (out[n], k) for k, r in enumerate(load)}


def right(work, held_a, held_e, grad_v, earlier=None, last=False):
    n = len(work)

    def body(*refs):
        g_ref, rest = refs[3 * n], refs[3 * n + 1 :]
        given, outs = (rest[:3], rest[3:]) if earlier else ((), rest)
        tmp, q, gram = (x[...] for x in given) if earlier else (0.0, 0.0, 0.0)
        for i, (r, _, entry) in enumerate(work):
            block, a_ref, e_ref = refs[3 * i : 3 * i + 3]
            a, e = a_ref[held_a[r][1]], e_ref[held_e[r][1]]
            p = split3(block[...] if entry is None else block[entry])
            tmp = tmp + fold3(lax.dot_general(p, a, NT, preferred_element_type=F32))
            q = q + fold3(jnp.dot(p, e, preferred_element_type=F32))
            gram = gram + lax.dot_general(p, p, NT, preferred_element_type=F32)
        if last:
            q = q + fold3(jnp.dot(split3(tmp), g_ref[...], preferred_element_type=F32))
            outs[0][...] = q
            outs[1][...] = gram
        else:
            outs[0][...] = tmp
            outs[1][...] = q
            outs[2][...] = gram

    shapes = [
        jax.ShapeDtypeStruct((RANK, TOK), F32),
        jax.ShapeDtypeStruct((RANK, COLS), F32),
        jax.ShapeDtypeStruct((TRI, TRI), F32),
    ]
    if last:
        shapes = shapes[1:]
    args = [x for r, array, _ in work for x in (array, held_a[r][0], held_e[r][0])]
    args += [grad_v, *(earlier or ())]
    return pl.pallas_call(
        body,
        out_shape=shapes,
        in_specs=[VM] * len(args),
        out_specs=[VM] * len(shapes),
        compiler_params=params(8),
        cost_estimate=cost(2 * n * 256 * COLS * (TOK + COLS)),
        name="right_last" if last else "right_part",
    )(*args)


def orthonormal_body(gram_ref, dither_ref, *refs):
    blocks, theirs, p3_ref, inv_ref, scale_ref = refs[: HALF + 1], *refs[HALF + 1 :]
    scale_ref[...] = 1.0 + (dither_ref[...].astype(F32) / 65536.0 - 0.5) / 4.0
    wide = fold3(gram_ref[...])
    gram = wide[:, :RANK] + wide[:, RANK : 2 * RANK] + wide[:, 2 * RANK :]
    rows = lax.broadcasted_iota(jnp.int32, (RANK, RANK), 0)
    cols = lax.broadcasted_iota(jnp.int32, (RANK, RANK), 1)
    eye = (rows == cols).astype(F32)
    work = jnp.concatenate([gram, eye], axis=1)
    wide = (RANK, 2 * RANK)
    below = lax.broadcasted_iota(jnp.int32, wide, 0)
    for k in range(0, RANK, 8):
        col = [jnp.broadcast_to(work[:, k + i : k + i + 1], wide) for i in range(8)]
        row = [work[k + i : k + i + 1, :] for i in range(8)]
        factor = []
        for i in range(8):
            f = jnp.where(below > k + i, col[i] / col[i][k + i : k + i + 1, :], 0.0)
            factor.append(f)
            for j in range(i + 1, 8):
                col[j] = col[j] - f * col[j][k + i : k + i + 1, :]
                row[j] = row[j] - f[k + j : k + j + 1, :] * row[i]
        for f, r in zip(factor, row):
            work = work - f * r
    diag = jnp.sum(work[:, :RANK] * eye, axis=1, keepdims=True)
    inv = work[:, RANK:] / jnp.sqrt(diag)
    inv_ref[...] = inv
    for k in range(NBLK):
        block = theirs[k - HALF - 1] if k > HALF else blocks[k][...]
        p = jnp.dot(inv, block, precision=HIGH, preferred_element_type=F32)
        hi = p.astype(BF16).astype(F32)
        r = p - hi
        mid = r.astype(BF16).astype(F32)
        stacked = jnp.concatenate([hi, mid, r - mid, jnp.zeros_like(p)], axis=0)
        p3_ref[k] = stacked.T.astype(BF16)


def orthonormal(gram, dither, blocks, theirs):
    return pl.pallas_call(
        orthonormal_body,
        out_shape=(
            pltpu.VMEM((NBLK, COLS, 4 * RANK), BF16),
            jax.ShapeDtypeStruct((RANK, RANK), F32),
            jax.ShapeDtypeStruct((RANK, COLS), F32),
        ),
        in_specs=[VM] * (4 + HALF),
        out_specs=(VM, VM, VM),
        compiler_params=params(8),
        cost_estimate=cost(1 << 31),
        name="orthonormal",
    )(gram, dither, *blocks, theirs)


def update_body(me_ref, a_ref, b_ref, c_ref, d_ref, inv_ref, scale_ref, p3_ref, *rest):
    mem = rest[:NBLK]
    qf_ref, out_hbm, stage, sem = rest[NBLK:]
    total = (a_ref[...] + b_ref[...]) + (c_ref[...] + d_ref[...])
    qmat = jnp.dot(inv_ref[...], total, precision=HIGH, preferred_element_type=F32) / WORKERS
    qt = (qmat * scale_ref[...]).astype(BF16)
    qf_ref[...] = qt
    q3 = jnp.concatenate([qt, qt, qt, jnp.zeros((RANK, COLS), BF16)], axis=0)
    copies = []
    half = COLS // 2
    for k, r in enumerate(ORDER):
        for i in range(2):
            rows = pl.ds(i * half, half)
            approx = jnp.dot(p3_ref[k, rows], q3, preferred_element_type=F32)
            stage[k, rows] = (mem[k][rows] - approx).astype(BF16)
            at = pl.ds(pl.multiple_of(rows_of(me_ref[0], r) + i * half, half), half)
            copies.append(
                pltpu.make_async_copy(stage.at[k, rows], out_hbm.at[at, :], sem.at[2 * k + i])
            )
            copies[-1].start()
    for c in copies:
        c.wait()


def update(me, parts, inv, dither, p3, memory):
    return pl.pallas_call(
        update_body,
        out_shape=(
            jax.ShapeDtypeStruct((RANK, COLS), BF16),
            jax.ShapeDtypeStruct((D, COLS), BF16),
        ),
        in_specs=[SM] + [VM] * (len(parts) + 3 + NBLK),
        out_specs=(VM, ANY),
        scratch_shapes=[
            pltpu.VMEM((NBLK, COLS, COLS), BF16),
            pltpu.SemaphoreType.DMA((2 * NBLK,)),
        ],
        compiler_params=params(16),
        cost_estimate=cost(2 * D * COLS * 256, 7 * MB),
        name="update",
    )(me, *parts, inv, dither, p3, *memory)


def sum_after(parts, after):
    n = len(parts)

    def body(*refs):
        total = refs[0][...]
        for x in refs[1:n]:
            total = total + x[...]
        refs[-1][...] = total

    return pl.pallas_call(
        body,
        out_shape=jax.ShapeDtypeStruct((RANK, COLS), F32),
        in_specs=[VM] * n + [ANY] * len(after),
        out_specs=VM,
        compiler_params=params(8),
        cost_estimate=cost(1000),
        name="sum_after",
    )(*parts, *after)


def stack_after(parts, after):
    n = len(parts)

    def body(*refs):
        for i in range(n):
            refs[-1][i] = refs[i][...]

    return pl.pallas_call(
        body,
        out_shape=jax.ShapeDtypeStruct((n, RANK, COLS), F32),
        in_specs=[VM] * n + [ANY] * len(after),
        out_specs=VM,
        compiler_params=params(8),
        cost_estimate=cost(1000),
        name="stack_after",
    )(*parts, *after)


def place(y, x, z, core):
    return ((y * 4 + x) * 4 + z) * 2 + core


def exchange(v, axes, r):
    pairs = []
    for source in range(128):
        at = {"y": source >> 5, "x": source >> 3 & 3, "z": source >> 1 & 3}
        at[axes[source & 1]] ^= r
        pairs.append((source, place(core=source & 1, **at)))
    return lax.ppermute(v, ("dp", "tensor"), pairs)


def ring(v, axes):
    return [exchange(v, axes, r) for r in RING]


def core(v):
    return lax.ppermute(v, ("dp", "tensor"), [(i, i ^ 1) for i in range(128)])


def per_device(acts, out_grad, error, q_seed, dither):
    me = lax.axis_index(("dp", "tensor")).astype(jnp.int32).reshape(1)
    acts = pltpu.with_memory_space_constraint(acts, pltpu.HBM)
    error = pltpu.with_memory_space_constraint(error, pltpu.HBM)
    out_grad = pltpu.with_memory_space_constraint(out_grad, pltpu.HBM)
    seed = pltpu.with_memory_space_constraint(q_seed.T, pltpu.HBM)

    away, held_e, grad_v, qt = left_away(me, error, out_grad, seed)
    came = core(away)
    kept, held_a, more_e = left_kept(me, acts, error, qt)
    held_e |= more_e
    part, t3 = left_sum(held_a[2][0], kept, away, came)
    from_ring = [exchange(part[r - 1], OWNER, r) for r in RING]
    own, more_a, more_e = left_own(me, acts, error, qt, t3, came, part)
    held_a |= more_a
    held_e |= more_e
    memory = {}

    def memory_of(rs, after, load=()):
        blocks, more = memory_blocks(rs, held_a, held_e, grad_v, after, load, me, acts)
        memory.update(blocks)
        held_a.update(more)

    memory_of((2,), part)
    own = sum_after([own, *from_ring], [memory[2]])

    from_ring = ring(own, SECOND)
    memory_of((0,), own, (1, 3, 5))
    own = sum_after([own, *from_ring], [memory[0]])
    from_ring = ring(own, THIRD)
    memory_of((4, 1), own, (7,))
    own = sum_after([own, *from_ring], [memory[4]])

    other = core(own)
    mine = ring(own, OWNER)
    memory_of((6,), own)
    held = (held_a, held_e, grad_v)
    early = right([(0, own, None), (1, other, None)], *held)
    early = right([(2 * RING[2], mine[2], None)], *held, early)
    theirs = core(stack_after(mine, [early[0], memory[6]]))
    mid = right([(2 * r, x, None) for r, x in zip(RING[:2], mine)], *held, early)
    q, gram = right([(2 * r + 1, theirs, i) for i, r in enumerate(RING)], *held, mid, True)

    from_ring = ring(q, DP_FIRST)
    p3, inv, scale = orthonormal(gram, dither.T, [own, other, *mine], theirs)
    memory_of((3,), q)
    q = sum_after([q, *from_ring], [inv, memory[3]])
    from_ring = ring(q, DP_SECOND)
    memory_of((5, 7), q)
    q_factor, new_error = update(me, [q, *from_ring], inv, scale, p3, [memory[r] for r in ORDER])
    return (q_factor.T, new_error)


def solution(mesh):
    in_specs = (
        P("dp", None),
        P("dp", "tensor"),
        P("dp", "tensor"),
        P("tensor", None),
        P("tensor", None),
    )
    out_specs = (P("tensor", None), P("dp", "tensor"))
    return jax.shard_map(
        per_device, mesh=mesh, in_specs=in_specs, out_specs=out_specs, check_vma=False
    )
```
